512 devices in a mesh: grp: 8 (over x, core), leaf: 64 (over y, z).
Axes of the slice: x: 4, y: 8, z: 8, core: 2. Of those that a mesh axis runs over, the one named last changes fastest.
Arguments:
- points: bfloat16 [262144, 64], P(('grp', 'leaf')), may hold values from -0.75 to 0.75
- weights: bfloat16 [262144, 32], P(('grp', 'leaf')), may hold values from -0.0625 to 0.0625
- interp: bfloat16 [262144, 1024], P(('grp', 'leaf')), may hold values from -0.03125 to 0.03125
- near_leaf: int32 [512, 16], P('grp'), may hold values from 0 to 63, as said below
- near_count: int32 [512], P('grp'), may hold values from 1 to 16, as said below
- skel_index: int32 [8, 1024], P('grp'), may hold values from 0 to 32767, as said below
Outputs:
- potential: float32 [262144, 32], P(('grp', 'leaf'))
The draws below stay inside these ranges and needn't reach their ends.
Inputs may be any that keep to these rules, and one draw needn't show every extreme that they name: `near_leaf`: each row holds distinct leaves; the first entry is the leaf itself. `near_count`: in every group some leaf uses all 16 slots. `skel_index`: each row holds distinct point numbers.
All inputs are finite; a program needn't handle non-finite values.
Results may differ from the reference program's by a relative error of at most 0.0038.
Values may be sent and summed in bfloat16 or wider, within the bound.
A program may use at most 64 MiB of HBM per device.

```python
import jax
import jax.numpy as jnp
from jax import lax

F = 64
R = 32
LEAF_PTS = 512
KN = 16
GS = 1024
NLEAVES = 512
GPTS = 32768
NPTS = 262144
N_GRP = 8
N_LEAF = 64


def draw_near_count(key, part):
    key = jax.random.fold_in(key, 1)
    key_a, key_b, key_c = jax.random.split(key, 3)
    base = jax.random.randint(key_a, (NLEAVES,), 1, 9)
    boost = jax.random.randint(key_b, (NLEAVES,), 0, 4)
    counts = jnp.minimum(KN, base * (1 + 2 * (boost == 3).astype(jnp.int32)))
    chosen = jax.random.randint(key_c, (N_GRP,), 0, N_LEAF)
    index = jnp.arange(NLEAVES, dtype=jnp.int32)
    full = index % N_LEAF == chosen[index // N_LEAF]
    return jnp.where(full, KN, counts).astype(jnp.int32)


def draw_near_leaf(key, part):
    key = jax.random.fold_in(key, 2)
    keys = jax.random.split(key, NLEAVES)
    others = jax.vmap(lambda k: jax.random.permutation(k, N_LEAF - 1))(keys)
    offsets = jnp.concatenate([jnp.zeros((NLEAVES, 1), jnp.int32), 1 + others[:, :KN - 1].astype(jnp.int32)], axis=1)
    index = jnp.arange(NLEAVES, dtype=jnp.int32)
    return ((index % N_LEAF)[:, None] + offsets) % N_LEAF


def draw_skel_index(key, part):
    key = jax.random.fold_in(key, 3)
    keys = jax.random.split(key, N_GRP)
    chosen = jax.vmap(lambda k: jax.random.permutation(k, GPTS))(keys)
    return chosen[:, :GS].astype(jnp.int32)


def shard_levels(rng, extent, shards, least, largest):
    factor_of = 1.0
    for dim, shards_of in shards:
        steps = jax.random.uniform(jax.random.fold_in(jax.random.fold_in(rng, 6), dim), (shards_of,), jnp.float32, least / len(shards), largest / len(shards))
        factor_of = factor_of * jnp.repeat(jnp.exp(steps), extent[dim] // shards_of).reshape((-1,) + (1,) * (len(extent) - 1 - dim))
    return factor_of


def normal_values(own_key, shape, deviation, bound, shards=(), kind=jnp.bfloat16):
    loudness = shard_levels(own_key, shape, shards, -0.22, 0.18) if shards else 1.0
    values = jax.random.normal(own_key, shape, jnp.float32) * deviation * loudness
    return jnp.minimum(jnp.maximum(values, -bound), bound).astype(kind)


def setup_inputs(seed: int = 0) -> dict:
    key_of = jax.random.split(jax.random.key(seed), 7)
    points = normal_values(key_of[0], (NPTS, F), 0.125, 0.75, ((0, 512),))
    weights = normal_values(key_of[1], (NPTS, R), (KN * LEAF_PTS) ** -0.5, 0.0625, ((0, 512),))
    interp = normal_values(key_of[2], (NPTS, GS), (N_LEAF * LEAF_PTS) ** -0.5, 0.03125, ((0, 512),))
    near_leaf = draw_near_leaf(jax.random.fold_in(key_of[6], 71), 0)
    near_count = draw_near_count(jax.random.fold_in(key_of[6], 71), 0)
    skel_index = draw_skel_index(jax.random.fold_in(key_of[6], 71), 0)
    return dict(points=points, weights=weights, interp=interp, near_leaf=near_leaf, near_count=near_count, skel_index=skel_index)


GAMMA = 0.5


def kernel_apply(targets, sources, source_wts):
    tnorm = jnp.sum(targets.astype(jnp.float32) ** 2, axis=1)
    snorm = jnp.sum(sources.astype(jnp.float32) ** 2, axis=1)
    cross = jnp.dot(targets, sources.T, preferred_element_type=jnp.float32)
    kern = jnp.exp(-GAMMA * (tnorm[:, None] + snorm[None, :] - 2.0 * cross)).astype(jnp.bfloat16)
    return jnp.dot(kern, source_wts, preferred_element_type=jnp.float32)


def reference(points, weights, interp, near_leaf, near_count, skel_index):
    pts = points.reshape(N_GRP, N_LEAF, LEAF_PTS, F)
    wts = weights.reshape(N_GRP, N_LEAF, LEAF_PTS, R)
    group_pts = points.reshape(N_GRP, GPTS, F)
    skel_pts = jnp.take_along_axis(group_pts, skel_index[:, :, None], axis=1)
    skel_wts = jnp.einsum("gps,gpr->gsr", interp.reshape(N_GRP, GPTS, GS).astype(jnp.float32),
                          weights.reshape(N_GRP, GPTS, R).astype(jnp.float32))
    skel_b = skel_wts.astype(jnp.bfloat16)

    def one_leaf(index):
        group = index // N_LEAF
        target = index % N_LEAF
        own = pts[group, target]

        def near_step(slot, total):
            source = near_leaf[index, slot]
            piece = kernel_apply(own, pts[group, source], wts[group, source])
            return total + jnp.where(slot < near_count[index], piece, jnp.zeros_like(piece))

        total = lax.fori_loop(0, KN, near_step, jnp.zeros((LEAF_PTS, R), jnp.float32))

        def far_step(other, total):
            piece = kernel_apply(own, skel_pts[other], skel_b[other])
            return total + jnp.where(other != group, piece, jnp.zeros_like(piece))

        return lax.fori_loop(0, N_GRP, far_step, total)

    result = lax.map(one_leaf, jnp.arange(NLEAVES, dtype=jnp.int32))
    return result.reshape(NPTS, R)
```

```python
import functools
import heapq

import jax
import jax.numpy as jnp
from jax import lax
from jax.experimental import pallas as pl
from jax.experimental.pallas import tpu as pltpu
from jax.sharding import PartitionSpec as P

MESH = pl.DeviceIdType.MESH
BF, F32 = jnp.bfloat16, jnp.float32
SIDE = 8
PTS, FEAT, COLS, SKEL, SLOTS = 512, 64, 32, 1024, 16
ROWS = FEAT + COLS
HALF = ROWS // 2
PIECE = SKEL // SIDE

FIRST = ((4, 3), (3, 4))


def second(o):
    return (4, 3) if o & 1 else (3, 4)


def hops(half, o1, o2):
    out = []
    if o2 == 0:
        if o1 <= 0 and -o1 < FIRST[half][0]:
            out.append((0, 1))
        if o1 >= 0 and o1 < FIRST[half][1]:
            out.append((0, -1))
        out += [(1, 1), (1, -1)]
    else:
        plus, minus = second(o1)
        if o2 < 0 and -o2 < plus:
            out.append((1, 1))
        if o2 > 0 and o2 < minus:
            out.append((1, -1))
    return out


def schedule():
    free, events, order, count = {}, [], [], 0

    def forward(now, half, o1, o2):
        nonlocal count
        for leg, sign in hops(half, o1, o2):
            link = ((half + leg) % 2, sign)
            begin = max(now, free.get(link, 0.0))
            free[link] = begin + 1.0
            count += 1
            seen = (o1 - sign, o2) if leg == 0 else (o1, o2 - sign)
            heapq.heappush(events, (begin + 2.0, count, half) + seen)

    for half in (0, 1):
        forward(0.0, half, 0, 0)
    while events:
        now, _, half, o1, o2 = heapq.heappop(events)
        order.append((half, o1, o2))
        forward(now, half, o1, o2)
    return order


def slot_of(half, o1, o2):
    oz, oy = (o1, o2) if half == 0 else (o2, o1)
    return (oy % SIDE) * SIDE + oz % SIDE


def split3(v):
    hi = v.astype(BF).astype(F32)
    mid = (v - hi).astype(BF).astype(F32)
    return hi, mid, v - hi - mid


def aug_rows(v, first):
    hi, mid, lo = split3(v)
    row = lax.broadcasted_iota(jnp.int32, (16, v.shape[1]), 0)
    k = row - 3 * first
    terms = jnp.where(k == 0, hi, jnp.where(k == 1, mid, lo))
    mine = (k >= 0) & (k < 3)
    return jnp.where(mine, terms, jnp.where(row < 6, 1.0, 0.0)).astype(BF)


def half_norm(xt):
    xf = xt.astype(F32)
    return -0.5 * jnp.sum(xf * xf, axis=0, keepdims=True)


def kernel(
    near_ref, count_ref, skel_idx, pts_ref, wts_ref, interp_ref, out_ref,
    gat, interp_v, part, got_z, mid, got_y, skel, lhs, acc,
    loc, g_send, g_recv, s_send, s_recv, x_recv,
):
    grp, leaf = lax.axis_index("grp"), lax.axis_index("leaf")
    x, core = grp // 2, grp % 2
    y, z = leaf // SIDE, leaf % SIDE

    def at_leaf(oy, oz):
        return (grp, ((y + oy) % SIDE) * SIDE + (z + oz) % SIDE)

    def at_grp(ox, oc):
        return (((x + ox) % 4) * 2 + (core + oc) % 2, leaf)

    own = [
        pltpu.make_async_copy(pts_ref, gat.at[0, pl.ds(0, FEAT)], loc.at[0]),
        pltpu.make_async_copy(wts_ref, gat.at[0, pl.ds(FEAT, COLS)], loc.at[1]),
        pltpu.make_async_copy(interp_ref, interp_v, loc.at[2]),
    ]
    for c in own:
        c.start()
    barrier = pltpu.get_barrier_semaphore()
    peers = [at_leaf(0, o) for o in range(1, SIDE)] + [at_leaf(o, 0) for o in range(1, SIDE)]
    peers += [at_grp(o, 0) for o in range(1, 4)] + [at_grp(0, 1)]
    for peer in peers:
        pl.semaphore_signal(barrier, inc=1, device_id=peer, device_id_type=MESH)
    own[0].wait()
    own[1].wait()
    pl.semaphore_wait(barrier, len(peers))

    def remote(src, dst, send, recv, peer):
        pltpu.make_async_remote_copy(
            src_ref=src, dst_ref=dst, send_sem=send, recv_sem=recv,
            device_id=peer, device_id_type=MESH,
        ).start()

    def forward(half, o1, o2):
        here = slot_of(half, o1, o2)
        rows = pl.ds(half * HALF, HALF)
        for leg, sign in hops(half, o1, o2):
            there = slot_of(half, *((o1 - sign, o2) if leg == 0 else (o1, o2 - sign)))
            peer = at_leaf(0, sign) if (half + leg) % 2 == 0 else at_leaf(sign, 0)
            remote(gat.at[here, rows], gat.at[there, rows], g_send, g_recv.at[half, there], peer)

    def arrive(half, o1, o2):
        here = slot_of(half, o1, o2)
        ref = gat.at[here, pl.ds(half * HALF, HALF)]
        pltpu.make_async_copy(ref, ref, g_recv.at[half, here]).wait()
        forward(half, o1, o2)

    def whole(ref, sem):
        pltpu.make_async_copy(ref, ref, sem).wait()

    for half in (0, 1):
        forward(half, 0, 0)

    def skel_part():
        own[2].wait()
        index = skel_idx[...] - leaf * PTS
        pick = lax.broadcasted_iota(jnp.int32, (PTS, SKEL), 0) == index
        pts = jnp.dot(gat[0, :FEAT], pick.astype(BF), preferred_element_type=F32).astype(BF)
        wts = jnp.dot(gat[0, FEAT:], interp_v[...], preferred_element_type=F32)
        hi = wts.astype(BF)
        lo = (wts - hi.astype(F32)).astype(BF)
        for k in range(SIDE):
            cols = slice(k * PIECE, (k + 1) * PIECE)
            part[k, :FEAT] = pts[:, cols]
            part[k, FEAT:ROWS] = hi[:, cols]
            part[k, ROWS:] = lo[:, cols]
        for o in range(1, SIDE):
            remote(part.at[(z + o) % SIDE], got_z.at[7 - o], s_send.at[0], s_recv.at[0], at_leaf(0, o))

    def total(first, got):
        def add(k, carry):
            p, w = carry
            v = got[k].astype(F32)
            return p + v[:FEAT], w + v[FEAT:ROWS] + v[ROWS:]

        v = first.astype(F32)
        return lax.fori_loop(0, SIDE - 1, add, (v[:FEAT], v[FEAT:ROWS] + v[ROWS:]))

    def skel_z():
        whole(got_z, s_recv.at[0])
        p, w = total(part[z], got_z)
        hi = w.astype(BF)
        mid[:FEAT] = p.astype(BF)
        mid[FEAT:ROWS] = hi
        mid[ROWS:] = (w - hi.astype(F32)).astype(BF)
        for o in range(1, SIDE):
            remote(mid, got_y.at[7 - o], s_send.at[1], s_recv.at[1], at_leaf(o, 0))

    def skel_y():
        whole(got_y, s_recv.at[1])
        p, w = total(mid[...], got_y)
        skel[0, z, :FEAT] = p.astype(BF)
        skel[0, z, FEAT:] = w.astype(BF)
        for o in range(1, SIDE):
            remote(skel.at[0, z], skel.at[0, z], s_send.at[2], s_recv.at[2], at_leaf(0, o))

    def skel_own():
        whole(skel.at[0, pl.ds(0, 7)], s_recv.at[2])
        for o in (1, 3, 2):
            there = ((4 - o) % 4) * 2
            remote(skel.at[0], skel.at[there], s_send.at[3], x_recv.at[there], at_grp(o, 0))
        remote(skel.at[0], skel.at[1], s_send.at[3], x_recv.at[1], at_grp(0, 1))

    def skel_x(o):
        whole(skel.at[2 * o], x_recv.at[2 * o])
        remote(skel.at[2 * o], skel.at[2 * o + 1], s_send.at[3], x_recv.at[2 * o + 1], at_grp(0, 1))

    def block(xs, ws):
        rhs = jnp.concatenate([xs, aug_rows(half_norm(xs), 0)], axis=0)
        arg = jnp.dot(lhs[...], rhs, preferred_element_type=F32)
        kern = jnp.exp(arg).astype(BF)
        acc[...] += lax.dot_general(kern, ws, (((1,), (1,)), ((), ())), preferred_element_type=F32)

    def targets():
        xt = gat[0, :FEAT]
        rows = jnp.concatenate([xt, aug_rows(half_norm(xt), 1)], axis=0)
        pad = jnp.zeros((128 - rows.shape[0], PTS), F32)
        turned = jnp.concatenate([rows.astype(F32), pad], axis=0).T
        lhs[...] = turned[:, :FEAT + 16].astype(BF)
        acc[...] = jnp.zeros_like(acc)

    def far(rel):
        whole_it = rel % 2 == 1
        if whole_it:
            whole(skel.at[rel], x_recv.at[rel])

        @pl.loop(0, 2)
        def _(k):
            both = jnp.concatenate([skel[rel, 4 * k + i] for i in range(4)], axis=1)
            block(both[:FEAT], both[FEAT:])

    order = schedule()
    steps = {
        0: [skel_part], 8: [targets], 14: [skel_z], 26: [skel_y], 40: [skel_own],
        66: [lambda: far(1)], 74: [lambda: skel_x(1)], 76: [lambda: skel_x(3)],
        82: [lambda: far(2)], 88: [lambda: far(6)], 92: [lambda: skel_x(2)],
        94: [lambda: far(3)], 100: [lambda: far(7)], 106: [lambda: far(4)], 112: [lambda: far(5)],
    }
    for i, event in enumerate(order):
        for f in steps.get(i, ()):
            f()
        arrive(*event)

    mine = count_ref[leaf]

    @pl.loop(0, SLOTS)
    def _(k):
        source = near_ref[k, leaf]
        sy = (source // SIDE + SIDE - y) % SIDE
        sz = (source % SIDE + SIDE - z) % SIDE
        got = gat[sy * SIDE + sz]
        used = jnp.where(k < mine, 1.0, 0.0).astype(F32)
        block(got[:FEAT], (got[FEAT:].astype(F32) * used).astype(BF))

    pad = jnp.zeros((PTS, 128 - COLS), F32)
    out_ref[...] = jnp.concatenate([acc[...], pad], axis=1).T[:COLS]

    sent = gat.at[pl.ds(0, 63)]
    pltpu.make_async_copy(sent, sent, g_send).wait()
    for i, ref in enumerate((got_z, got_y, skel.at[0, pl.ds(0, 7)], skel.at[pl.ds(0, 7)])):
        whole(ref, s_send.at[i])


def per_device(points, weights, interp, near_leaf, near_count, skel_index):
    flops = 2 * 30 * PTS * PTS * (FEAT + 16 + COLS) + 2 * PTS * SKEL * ROWS
    out = pl.pallas_call(
        kernel,
        out_shape=jax.ShapeDtypeStruct((COLS, PTS), F32),
        in_specs=[
            pl.BlockSpec(memory_space=pltpu.SMEM),
            pl.BlockSpec(memory_space=pltpu.SMEM),
            pl.BlockSpec(memory_space=pltpu.VMEM),
            pl.BlockSpec(memory_space=pl.ANY),
            pl.BlockSpec(memory_space=pl.ANY),
            pl.BlockSpec(memory_space=pl.ANY),
        ],
        out_specs=pl.BlockSpec(memory_space=pltpu.VMEM),
        scratch_shapes=[
            pltpu.VMEM((64, ROWS, PTS), BF),
            pltpu.VMEM((PTS, SKEL), BF),
            pltpu.VMEM((SIDE, ROWS + COLS, PIECE), BF),
            pltpu.VMEM((SIDE - 1, ROWS + COLS, PIECE), BF),
            pltpu.VMEM((ROWS + COLS, PIECE), BF),
            pltpu.VMEM((SIDE - 1, ROWS + COLS, PIECE), BF),
            pltpu.VMEM((8, SIDE, ROWS, PIECE), BF),
            pltpu.VMEM((PTS, FEAT + 16), BF),
            pltpu.VMEM((PTS, COLS), F32),
            pltpu.SemaphoreType.DMA((3,)),
            pltpu.SemaphoreType.DMA,
            pltpu.SemaphoreType.DMA((2, 64)),
            pltpu.SemaphoreType.DMA((4,)),
            pltpu.SemaphoreType.DMA((3,)),
            pltpu.SemaphoreType.DMA((8,)),
        ],
        cost_estimate=pl.CostEstimate(
            flops=flops, bytes_accessed=2 * PTS * SKEL, transcendentals=30 * PTS * PTS
        ),
        compiler_params=pltpu.CompilerParams(
            collective_id=0, has_side_effects=True, vmem_limit_bytes=48 * 1024 * 1024
        ),
    )(near_leaf.T, near_count, skel_index, points.T, weights.T, interp)
    return out.T


def solution(mesh):
    placed = (
        P(("grp", "leaf"), None),
        P(("grp", "leaf"), None),
        P(("grp", "leaf"), None),
        P("grp", None),
        P("grp"),
        P("grp", None),
    )
    return jax.shard_map(
        per_device, mesh=mesh, in_specs=placed, out_specs=P(("grp", "leaf"), None), check_vma=False
    )
```

```python
import functools
import heapq

import jax
import jax.numpy as jnp
from jax import lax
from jax.experimental import pallas as pl
from jax.experimental.pallas import tpu as pltpu
from jax.sharding import PartitionSpec as P

MESH = pl.DeviceIdType.MESH
BF, F32 = jnp.bfloat16, jnp.float32
SIDE = 8
PTS, FEAT, COLS, SKEL, SLOTS = 512, 64, 32, 1024, 16
ROWS = FEAT + COLS
HALF = ROWS // 2
PIECE = SKEL // SIDE

FIRST = ((4, 3), (3, 4))


def second(o):
    return (4, 3) if o & 1 else (3, 4)


def hops(half, o1, o2):
    out = []
    if o2 == 0:
        if o1 <= 0 and -o1 < FIRST[half][0]:
            out.append((0, 1))
        if o1 >= 0 and o1 < FIRST[half][1]:
            out.append((0, -1))
        out += [(1, 1), (1, -1)]
    else:
        plus, minus = second(o1)
        if o2 < 0 and -o2 < plus:
            out.append((1, 1))
        if o2 > 0 and o2 < minus:
            out.append((1, -1))
    return out


CHUNK, HOP, LEAD, STAGE, PART = 0.98, 1.7, 2.0, 3.2, 2.2


def schedule():
    links = [(axis, sign) for axis in (0, 1) for sign in (1, -1)]
    free = {link: 0.0 for link in links}
    queue = {link: [] for link in links}
    arrivals, ready, program = [], [(0.0, 0, "part")], []
    count, now = 0, 0.0

    def left(half, o1, o2, leg, sign):
        reach = FIRST[half] if leg == 0 else second(o1)
        gone = abs(o1) if leg == 0 else abs(o2)
        return reach[0 if sign > 0 else 1] - gone + (4 if leg == 0 else 0)

    def enqueue(half, o1, o2):
        nonlocal count
        for leg, sign in hops(half, o1, o2):
            count += 1
            item = (-left(half, o1, o2, leg, sign), count, half, o1, o2, leg, sign)
            heapq.heappush(queue[((half + leg) % 2, sign)], item)

    def burst(share, after):
        nonlocal count
        end = now
        for axis, sign in links:
            free[axis, sign] = max(now, free[axis, sign]) + 8 * share[axis] * CHUNK
            end = max(end, free[axis, sign])
        count += 1
        heapq.heappush(ready, (end + STAGE, count, after))

    def at(delay, *names):
        nonlocal count
        for name in names:
            count += 1
            heapq.heappush(ready, (now + delay, count, name))

    for half in (0, 1):
        enqueue(half, 0, 0)
    while True:
        if arrivals and arrivals[0][0] <= now:
            _, _, half, o1, o2 = heapq.heappop(arrivals)
            program.append(("wait", half, o1, o2))
            now += 0.04
            enqueue(half, o1, o2)
            continue
        open_links = [k for k in links if queue[k] and free[k] - now <= LEAD]
        if open_links:
            link = min(open_links, key=lambda k: free[k])
            _, _, half, o1, o2, leg, sign = heapq.heappop(queue[link])
            program.append(("send", half, o1, o2, leg, sign))
            free[link] = max(now, free[link]) + CHUNK
            seen = (o1 - sign, o2) if leg == 0 else (o1, o2 - sign)
            count += 1
            heapq.heappush(arrivals, (free[link] + HOP, count, half) + seen)
            now += 0.03
            continue
        if ready and ready[0][0] <= now:
            name = heapq.heappop(ready)[2]
            program.append((name,))
            if name == "part":
                now += PART
                burst((1 / 3, 1 / 3), "sum1")
                at(0.0, "targets")
            elif name == "targets":
                now += 0.6
                at(0.0, "self")
            elif name == "sum1":
                now += 0.3
                burst((1 / 3, 1 / 3), "sum2")
            elif name == "sum2":
                now += 0.3
                burst((1 / 6, 1 / 3), "own")
            elif name == "own":
                at(2.5, "far1")
                at(6.0, "x1", "x3")
            elif name in ("x1", "x3"):
                at(0.5, "far" + {"x1": "2", "x3": "6"}[name])
                at(3.0, "far" + {"x1": "3", "x3": "7"}[name])
                if name == "x3":
                    at(4.2, "x2")
            elif name == "x2":
                at(0.2, "far4")
                at(3.0, "far5")
            else:
                now += 0.36 if name == "self" else 0.72
            continue
        times = [free[k] - LEAD for k in links if queue[k]]
        times += [arrivals[0][0]] if arrivals else []
        times += [ready[0][0]] if ready else []
        if not times:
            return program, now
        now = max(now + 1e-3, min(times))


def slot_of(half, o1, o2):
    oz, oy = (o1, o2) if half == 0 else (o2, o1)
    return (oy % SIDE) * SIDE + oz % SIDE


def split3(v):
    hi = v.astype(BF).astype(F32)
    mid = (v - hi).astype(BF).astype(F32)
    return hi, mid, v - hi - mid


def aug_rows(v, first):
    hi, mid, lo = split3(v)
    row = lax.broadcasted_iota(jnp.int32, (16, v.shape[1]), 0)
    k = row - 3 * first
    terms = jnp.where(k == 0, hi, jnp.where(k == 1, mid, lo))
    mine = (k >= 0) & (k < 3)
    return jnp.where(mine, terms, jnp.where(row < 6, 1.0, 0.0)).astype(BF)


def half_norm(xt):
    xf = xt.astype(F32)
    return -0.5 * jnp.sum(xf * xf, axis=0, keepdims=True)


def kernel(
    near_hbm, count_hbm, index_hbm, pts_ref, wts_ref, interp_ref, out_ref,
    gat, interp_v, near_ref, count_ref, index_v, part, got1, mid, got2, skel, lhs, acc,
    loc, g_send, g_recv, s_send, s_recv, x_recv,
):
    grp, leaf = lax.axis_index("grp"), lax.axis_index("leaf")
    x, core = grp // 2, grp % 2
    y, z = leaf // SIDE, leaf % SIDE

    def at_leaf(oy, oz):
        return (grp, ((y + oy + SIDE) % SIDE) * SIDE + (z + oz + SIDE) % SIDE)

    def at_grp(ox, oc):
        return (((x + ox) % 4) * 2 + (core + oc) % 2, leaf)

    barrier = pltpu.get_barrier_semaphore()
    peers = [at_leaf(0, o) for o in range(1, SIDE)] + [at_leaf(o, 0) for o in range(1, SIDE)]
    peers += [at_grp(1, 0), at_grp(3, 0), at_grp(0, 1)]
    for peer in peers:
        pl.semaphore_signal(barrier, inc=1, device_id=peer, device_id_type=MESH)
    own = [
        pltpu.make_async_copy(pts_ref, gat.at[0, pl.ds(0, FEAT)], loc.at[0]),
        pltpu.make_async_copy(wts_ref, gat.at[0, pl.ds(FEAT, COLS)], loc.at[1]),
        pltpu.make_async_copy(interp_ref, interp_v, loc.at[2]),
        pltpu.make_async_copy(index_hbm, index_v, loc.at[3]),
        pltpu.make_async_copy(near_hbm, near_ref, loc.at[4]),
        pltpu.make_async_copy(count_hbm, count_ref, loc.at[5]),
    ]
    for c in own:
        c.start()
    own[0].wait()
    own[1].wait()
    pl.semaphore_wait(barrier, len(peers))

    def remote(src, dst, send, recv, peer):
        pltpu.make_async_remote_copy(
            src_ref=src, dst_ref=dst, send_sem=send, recv_sem=recv,
            device_id=peer, device_id_type=MESH,
        ).start()

    def whole(ref, sem):
        pltpu.make_async_copy(ref, ref, sem).wait()

    def do_send(half, o1, o2, leg, sign):
        here = slot_of(half, o1, o2)
        there = slot_of(half, *((o1 - sign, o2) if leg == 0 else (o1, o2 - sign)))
        rows = pl.ds(half * HALF, HALF)
        peer = at_leaf(0, sign) if (half + leg) % 2 == 0 else at_leaf(sign, 0)
        remote(gat.at[here, rows], gat.at[there, rows], g_send, g_recv.at[half, there], peer)

    def do_wait(half, o1, o2):
        here = slot_of(half, o1, o2)
        whole(gat.at[here, pl.ds(half * HALF, HALF)], g_recv.at[half, here])

    def exchange(src_of, dst, stage):
        for o in range(1, SIDE):
            for kind in (0, 1):
                along_y = (kind + stage) % 2 == 0
                peer = at_leaf(o, 0) if along_y else at_leaf(0, o)
                remote(src_of(kind, o), dst.at[kind, 7 - o], s_send.at[stage, kind],
                       s_recv.at[stage, kind], peer)

    def do_part():
        own[2].wait()
        own[3].wait()
        index = index_v[...] - leaf * PTS
        pick = lax.broadcasted_iota(jnp.int32, (PTS, SKEL), 0) == index
        pts = jnp.dot(gat[0, :FEAT], pick.astype(BF), preferred_element_type=F32).astype(BF)
        wts = jnp.dot(gat[0, FEAT:], interp_v[...], preferred_element_type=F32)
        hi = wts.astype(BF)
        lo = (wts - hi.astype(F32)).astype(BF)
        for k in range(SIDE):
            cols = slice(k * PIECE, (k + 1) * PIECE)
            part[0, k] = pts[:, cols]
            part[1, k, :COLS] = hi[:, cols]
            part[1, k, COLS:] = lo[:, cols]
        place = (y, z)
        exchange(lambda kind, o: part.at[kind, (place[kind] + o) % SIDE], got1, 0)

    def total(kind, first, got):
        v = first.astype(F32)
        for k in range(SIDE - 1):
            v = v + got[kind, k].astype(F32)
        return v if kind == 0 else v[:COLS] + v[COLS:]

    def do_sum1():
        for kind in (0, 1):
            whole(got1.at[kind], s_recv.at[0, kind])
        mid[0] = total(0, part[0, y], got1).astype(BF)
        w = total(1, part[1, z], got1)
        hi = w.astype(BF)
        mid[1, :COLS] = hi
        mid[1, COLS:] = (w - hi.astype(F32)).astype(BF)
        exchange(lambda kind, o: mid.at[kind], got2, 1)

    def do_sum2():
        for kind in (0, 1):
            whole(got2.at[kind], s_recv.at[1, kind])
        skel[0, y, :FEAT] = total(0, mid[0], got2).astype(BF)
        skel[0, z, FEAT:] = total(1, mid[1], got2).astype(BF)
        p, w = skel.at[0, y, pl.ds(0, FEAT)], skel.at[0, z, pl.ds(FEAT, COLS)]
        for o in range(1, SIDE):
            remote(p, p, s_send.at[2, 0], s_recv.at[2, 0], at_leaf(o, 0))
            remote(w, w, s_send.at[2, 1], s_recv.at[2, 1], at_leaf(0, o))

    others = (skel.at[0, pl.ds(0, 7), pl.ds(0, FEAT)], skel.at[0, pl.ds(0, 7), pl.ds(FEAT, COLS)])

    def do_own():
        for kind in (0, 1):
            whole(others[kind], s_recv.at[2, kind])
        for dx in (1, 3):
            there = 2 * (4 - dx)
            remote(skel.at[0], skel.at[there], s_send.at[3, 0], x_recv.at[there], at_grp(dx, 0))
        remote(skel.at[0], skel.at[1], s_send.at[3, 0], x_recv.at[1], at_grp(0, 1))

    def do_x(dx):
        if dx != 2:
            whole(skel.at[2 * dx], x_recv.at[2 * dx])
            part_of = pl.ds(0 if dx == 1 else 4, 4)
            remote(skel.at[2 * dx, part_of], skel.at[4, part_of], s_send.at[3, 1],
                   x_recv.at[4 if dx == 1 else 8], at_grp(4 - dx, 0))
        else:
            whole(skel.at[4, pl.ds(0, 4)], x_recv.at[4])
            whole(skel.at[4, pl.ds(4, 4)], x_recv.at[8])
        remote(skel.at[2 * dx], skel.at[2 * dx + 1], s_send.at[3, 0], x_recv.at[2 * dx + 1], at_grp(0, 1))

    def block(xs, ws):
        rhs = jnp.concatenate([xs, aug_rows(half_norm(xs), 0)], axis=0)
        arg = jnp.dot(lhs[...], rhs, preferred_element_type=F32)
        kern = jnp.exp(arg).astype(BF)
        return lax.dot_general(kern, ws, (((1,), (1,)), ((), ())), preferred_element_type=F32)

    def do_targets():
        xt = gat[0, :FEAT]
        rows = jnp.concatenate([xt, aug_rows(half_norm(xt), 1)], axis=0)
        pad = jnp.zeros((128 - rows.shape[0], PTS), F32)
        turned = jnp.concatenate([rows.astype(F32), pad], axis=0).T
        lhs[...] = turned[:, :FEAT + 16].astype(BF)

    def do_self():
        acc[...] = block(gat[0, :FEAT], gat[0, FEAT:])

    def do_far(rel):
        if rel % 2 == 1:
            whole(skel.at[rel], x_recv.at[rel])
        both = jnp.concatenate([skel[rel, i] for i in range(SIDE)], axis=1)
        acc[...] += (block(both[:FEAT, :PTS], both[FEAT:, :PTS])
                     + block(both[:FEAT, PTS:], both[FEAT:, PTS:]))

    work = {"wait": do_wait, "send": do_send, "part": do_part, "sum1": do_sum1,
            "sum2": do_sum2, "own": do_own, "targets": do_targets, "self": do_self}
    for dx in (1, 2, 3):
        work["x%d" % dx] = functools.partial(do_x, dx)
    for rel in range(1, 8):
        work["far%d" % rel] = functools.partial(do_far, rel)
    for name, *args in schedule()[0]:
        work[name](*args)

    own[4].wait()
    own[5].wait()
    mine = count_ref[leaf]

    @pl.loop(0, SLOTS // 5)
    def _(i):
        add = jnp.zeros((PTS, COLS), F32)
        for j in range(5):
            k = 1 + 5 * i + j
            source = near_ref[k, leaf]
            sy = (source // SIDE + SIDE - y) % SIDE
            sz = (source % SIDE + SIDE - z) % SIDE
            got = gat[sy * SIDE + sz]
            used = jnp.where(k < mine, 1.0, 0.0).astype(F32)
            add = add + block(got[:FEAT], (got[FEAT:].astype(F32) * used).astype(BF))
        acc[...] += add

    pad = jnp.zeros((PTS, 128 - COLS), F32)
    out_ref[...] = jnp.concatenate([acc[...], pad], axis=1).T[:COLS]

    whole(gat.at[pl.ds(0, 63)], g_send)
    for kind in (0, 1):
        whole(got1.at[kind], s_send.at[0, kind])
        whole(got2.at[kind], s_send.at[1, kind])
        whole(others[kind], s_send.at[2, kind])
    whole(skel.at[pl.ds(0, 6)], s_send.at[3, 0])
    whole(skel.at[0], s_send.at[3, 1])


def per_device(points, weights, interp, near_leaf, near_count, skel_index):
    flops = 2 * 30 * PTS * PTS * (FEAT + 16 + COLS) + 2 * PTS * SKEL * ROWS
    out = pl.pallas_call(
        kernel,
        out_shape=jax.ShapeDtypeStruct((COLS, PTS), F32),
        in_specs=[pl.BlockSpec(memory_space=pltpu.HBM)] * 6,
        out_specs=pl.BlockSpec(memory_space=pltpu.VMEM),
        scratch_shapes=[
            pltpu.VMEM((64, ROWS, PTS), BF),
            pltpu.VMEM((PTS, SKEL), BF),
            pltpu.SMEM((SLOTS, 64), jnp.int32),
            pltpu.SMEM((64,), jnp.int32),
            pltpu.VMEM((1, SKEL), jnp.int32),
            pltpu.VMEM((2, SIDE, FEAT, PIECE), BF),
            pltpu.VMEM((2, SIDE - 1, FEAT, PIECE), BF),
            pltpu.VMEM((2, FEAT, PIECE), BF),
            pltpu.VMEM((2, SIDE - 1, FEAT, PIECE), BF),
            pltpu.VMEM((8, SIDE, ROWS, PIECE), BF),
            pltpu.VMEM((PTS, FEAT + 16), BF),
            pltpu.VMEM((PTS, COLS), F32),
            pltpu.SemaphoreType.DMA((6,)),
            pltpu.SemaphoreType.DMA,
            pltpu.SemaphoreType.DMA((2, 64)),
            pltpu.SemaphoreType.DMA((4, 2)),
            pltpu.SemaphoreType.DMA((3, 2)),
            pltpu.SemaphoreType.DMA((9,)),
        ],
        cost_estimate=pl.CostEstimate(
            flops=flops, bytes_accessed=2 * PTS * SKEL, transcendentals=30 * PTS * PTS
        ),
        compiler_params=pltpu.CompilerParams(
            collective_id=0, has_side_effects=True, vmem_limit_bytes=60 * 1024 * 1024
        ),
    )(near_leaf.T, near_count, skel_index, points.T, weights.T, interp)
    return out.T


def solution(mesh):
    placed = (
        P(("grp", "leaf"), None),
        P(("grp", "leaf"), None),
        P(("grp", "leaf"), None),
        P("grp", None),
        P("grp"),
        P("grp", None),
    )
    return jax.shard_map(
        per_device, mesh=mesh, in_specs=placed, out_specs=P(("grp", "leaf"), None), check_vma=False
    )
```

```python
import functools
import heapq

import jax
import jax.numpy as jnp
from jax import lax
from jax.experimental import pallas as pl
from jax.experimental.pallas import tpu as pltpu
from jax.sharding import PartitionSpec as P

MESH = pl.DeviceIdType.MESH
BF, F32 = jnp.bfloat16, jnp.float32
SIDE = 8
PTS, FEAT, COLS, SKEL, SLOTS = 512, 64, 32, 1024, 16
ROWS = FEAT + COLS
HALF = ROWS // 2
PIECE = SKEL // SIDE

FIRST = ((4, 3), (3, 4))


def second(o):
    return (4, 3) if o & 1 else (3, 4)


def hops(half, o1, o2):
    out = []
    if o2 == 0:
        if o1 <= 0 and -o1 < FIRST[half][0]:
            out.append((0, 1))
        if o1 >= 0 and o1 < FIRST[half][1]:
            out.append((0, -1))
        out += [(1, 1), (1, -1)]
    else:
        plus, minus = second(o1)
        if o2 < 0 and -o2 < plus:
            out.append((1, 1))
        if o2 > 0 and o2 < minus:
            out.append((1, -1))
    return out


CHUNK, HOP, LEAD, STAGE, PART = 0.98, 1.7, 2.0, 2.2, 2.2


def schedule():
    links = [(axis, sign) for axis in (0, 1) for sign in (1, -1)]
    free = {link: 0.0 for link in links}
    queue = {link: [] for link in links}
    arrivals, ready, program = [], [(0.0, 0, "part")], []
    count, now = 0, 0.0

    def left(half, o1, o2, leg, sign):
        reach = FIRST[half] if leg == 0 else second(o1)
        gone = abs(o1) if leg == 0 else abs(o2)
        return reach[0 if sign > 0 else 1] - gone + (4 if leg == 0 else 0)

    def enqueue(half, o1, o2):
        nonlocal count
        for leg, sign in hops(half, o1, o2):
            count += 1
            item = (-left(half, o1, o2, leg, sign), count, half, o1, o2, leg, sign)
            heapq.heappush(queue[((half + leg) % 2, sign)], item)

    def burst(share, after):
        nonlocal count
        end = now
        for axis, sign in links:
            free[axis, sign] = max(now, free[axis, sign]) + 8 * share[axis] * CHUNK
            end = max(end, free[axis, sign])
        count += 1
        heapq.heappush(ready, (end + STAGE, count, after))

    def at(delay, *names):
        nonlocal count
        for name in names:
            count += 1
            heapq.heappush(ready, (now + delay, count, name))

    for half in (0, 1):
        enqueue(half, 0, 0)
    while True:
        if arrivals and arrivals[0][0] <= now:
            _, _, half, o1, o2 = heapq.heappop(arrivals)
            program.append(("wait", half, o1, o2))
            now += 0.04
            enqueue(half, o1, o2)
            continue
        open_links = [k for k in links if queue[k] and free[k] - now <= LEAD]
        if open_links:
            link = min(open_links, key=lambda k: free[k])
            _, _, half, o1, o2, leg, sign = heapq.heappop(queue[link])
            program.append(("send", half, o1, o2, leg, sign))
            free[link] = max(now, free[link]) + CHUNK
            seen = (o1 - sign, o2) if leg == 0 else (o1, o2 - sign)
            count += 1
            heapq.heappush(arrivals, (free[link] + HOP, count, half) + seen)
            now += 0.03
            continue
        if ready and ready[0][0] <= now:
            name = heapq.heappop(ready)[2]
            program.append((name,))
            if name == "part":
                now += PART
                burst((1 / 3, 1 / 3), "sum1")
                at(0.0, "targets")
            elif name == "targets":
                now += 0.6
                at(0.0, "self")
            elif name == "sum1":
                now += 0.3
                burst((1 / 24, 1 / 24), "sum2")
            elif name == "sum2":
                now += 0.2
                burst((1 / 24, 1 / 48), "sum3")
            elif name == "sum3":
                burst((1 / 6, 1 / 3), "own")
            elif name == "own":
                at(3.0, "far1")
                at(4.2, "relay1", "relay3")
                at(6.2, "rest1", "rest3")
                at(8.6, "last")
            elif name in ("rest1", "rest3"):
                at(0.2, "far" + {"rest1": "2", "rest3": "6"}[name])
                at(2.5, "far" + {"rest1": "3", "rest3": "7"}[name])
            elif name == "last":
                at(0.2, "far4")
                at(2.5, "far5")
            elif name in ("relay1", "relay3"):
                pass
            else:
                now += 0.36 if name == "self" else 0.72
            continue
        times = [free[k] - LEAD for k in links if queue[k]]
        times += [arrivals[0][0]] if arrivals else []
        times += [ready[0][0]] if ready else []
        if not times:
            return program, now
        now = max(now + 1e-3, min(times))


def slot_of(half, o1, o2):
    oz, oy = (o1, o2) if half == 0 else (o2, o1)
    return (oy % SIDE) * SIDE + oz % SIDE


def split3(v):
    hi = v.astype(BF).astype(F32)
    mid = (v - hi).astype(BF).astype(F32)
    return hi, mid, v - hi - mid


def aug_rows(v, first):
    hi, mid, lo = split3(v)
    row = lax.broadcasted_iota(jnp.int32, (16, v.shape[1]), 0)
    k = row - 3 * first
    terms = jnp.where(k == 0, hi, jnp.where(k == 1, mid, lo))
    mine = (k >= 0) & (k < 3)
    return jnp.where(mine, terms, jnp.where(row < 6, 1.0, 0.0)).astype(BF)


def half_norm(xt):
    xf = xt.astype(F32)
    return -0.5 * jnp.sum(xf * xf, axis=0, keepdims=True)


def kernel(
    near_hbm, count_hbm, index_hbm, pts_ref, wts_ref, interp_ref, out_ref,
    gat, interp_v, near_ref, count_ref, index_v, part, got1, mid_p, mid_w, got_p, got_w, skel, lhs, acc,
    loc, g_send, g_recv, s_send, s_recv, x_recv,
):
    grp, leaf = lax.axis_index("grp"), lax.axis_index("leaf")
    x, core = grp // 2, grp % 2
    y, z = leaf // SIDE, leaf % SIDE

    def at_leaf(oy, oz):
        return (grp, ((y + oy + SIDE) % SIDE) * SIDE + (z + oz + SIDE) % SIDE)

    def at_grp(ox, oc):
        return (((x + ox) % 4) * 2 + (core + oc) % 2, leaf)

    barrier = pltpu.get_barrier_semaphore()
    peers = [at_leaf(0, o) for o in range(1, SIDE)] + [at_leaf(o, 0) for o in range(1, SIDE)]
    peers += [at_grp(1, 0), at_grp(3, 0), at_grp(0, 1)]
    for peer in peers:
        pl.semaphore_signal(barrier, inc=1, device_id=peer, device_id_type=MESH)
    own = [
        pltpu.make_async_copy(pts_ref, gat.at[0, pl.ds(0, FEAT)], loc.at[0]),
        pltpu.make_async_copy(wts_ref, gat.at[0, pl.ds(FEAT, COLS)], loc.at[1]),
        pltpu.make_async_copy(interp_ref, interp_v, loc.at[2]),
        pltpu.make_async_copy(index_hbm, index_v, loc.at[3]),
        pltpu.make_async_copy(near_hbm, near_ref, loc.at[4]),
        pltpu.make_async_copy(count_hbm, count_ref, loc.at[5]),
    ]
    for c in own:
        c.start()
    pl.semaphore_wait(barrier, len(peers))

    def remote(src, dst, send, recv, peer):
        pltpu.make_async_remote_copy(
            src_ref=src, dst_ref=dst, send_sem=send, recv_sem=recv,
            device_id=peer, device_id_type=MESH,
        ).start()

    def whole(ref, sem):
        pltpu.make_async_copy(ref, ref, sem).wait()

    def do_send(half, o1, o2, leg, sign):
        here = slot_of(half, o1, o2)
        there = slot_of(half, *((o1 - sign, o2) if leg == 0 else (o1, o2 - sign)))
        rows = pl.ds(half * HALF, HALF)
        peer = at_leaf(0, sign) if (half + leg) % 2 == 0 else at_leaf(sign, 0)
        parts = [(gat.at[here, rows], rows)]
        if here == 0 and half == 0:
            parts = [(pts_ref.at[rows], rows)]
        elif here == 0:
            last, below = pl.ds(HALF, FEAT - HALF), pl.ds(FEAT, COLS)
            parts = [(pts_ref.at[last], last), (wts_ref, below)]
        for src, place in parts:
            remote(src, gat.at[there, place], g_send, g_recv.at[half, there], peer)

    def do_wait(half, o1, o2):
        here = slot_of(half, o1, o2)
        whole(gat.at[here, pl.ds(half * HALF, HALF)], g_recv.at[half, here])

    def do_part():
        for c in own[:4]:
            c.wait()
        index = index_v[...] - leaf * PTS
        pick = lax.broadcasted_iota(jnp.int32, (PTS, SKEL), 0) == index
        pts = jnp.dot(gat[0, :FEAT], pick.astype(BF), preferred_element_type=F32).astype(BF)
        wts = jnp.dot(gat[0, FEAT:], interp_v[...], preferred_element_type=F32)
        hi = wts.astype(BF)
        lo = (wts - hi.astype(F32)).astype(BF)
        for k in range(SIDE):
            cols = slice(k * PIECE, (k + 1) * PIECE)
            part[0, k] = pts[:, cols]
            part[1, k, :COLS] = hi[:, cols]
            part[1, k, COLS:] = lo[:, cols]
        for o in range(1, SIDE):
            for kind, place in ((0, y), (1, z)):
                remote(part.at[kind, (place + o) % SIDE], got1.at[kind, 7 - o], s_send.at[0, kind],
                       s_recv.at[0, kind], peer_on(1 - kind, o))

    takes = ((z, 2, y, FEAT // 16), (y, 4, z, COLS // 16))

    def peer_on(kind, o):
        return at_leaf(0, o) if kind == 0 else at_leaf(o, 0)

    def total(kind, first, got):
        v = first.astype(F32)
        for k in range(SIDE - 1):
            v = v + got[kind, k].astype(F32)
        return v if kind == 0 else v[:COLS] + v[COLS:]

    def do_sum1():
        for kind in (0, 1):
            whole(got1.at[kind], s_recv.at[0, kind])
        mid_p[...] = total(0, part[0, y], got1).astype(BF)
        mid_w[...] = total(1, part[1, z], got1)
        for kind, (mid, got) in enumerate(((mid_p, got_p), (mid_w, got_w))):
            place, every, _, chunks = takes[kind]
            for c in range(chunks):
                off = (every * c - place + SIDE) % SIDE

                @pl.when(off != 0)
                def _():
                    remote(mid.at[pl.ds(16 * c, 16)], got.at[SIDE - 1 - off], s_send.at[1, kind],
                           s_recv.at[1, kind], peer_on(kind, off))

    def do_sum2():
        for kind, (mid, got) in enumerate(((mid_p, got_p), (mid_w, got_w))):
            place, every, piece, _ = takes[kind]

            @pl.when(place % every == 0)
            def _():
                whole(got, s_recv.at[1, kind])
                row = pl.multiple_of(place // every * 16, 16)
                v = mid[pl.ds(row, 16)].astype(F32)
                for k in range(SIDE - 1):
                    v = v + got[k].astype(F32)
                mine = pl.ds(pl.multiple_of(kind * FEAT + row, 16), 16)
                skel[0, piece, mine] = v.astype(BF)
                for o in range(1, SIDE):
                    ref = skel.at[0, piece, mine]
                    remote(ref, ref, s_send.at[2, kind], s_recv.at[2, kind], peer_on(kind, o))

    def by_count(kind, one, sem):
        place, every, _, chunks = takes[kind]
        for here in (0, 1):
            @pl.when((place % every == 0) if here else (place % every != 0))
            def _():
                whole(one(chunks - here), sem)

    def do_sum3():
        for kind in (0, 1):
            by_count(kind, lambda n: skel.at[0, 0, pl.ds(0, 16 * n)], s_recv.at[2, kind])
        p, w = skel.at[0, y, pl.ds(0, FEAT)], skel.at[0, z, pl.ds(FEAT, COLS)]
        for o in range(1, SIDE):
            remote(p, p, s_send.at[4, 0], s_recv.at[3, 0], at_leaf(o, 0))
            remote(w, w, s_send.at[4, 1], s_recv.at[3, 1], at_leaf(0, o))

    others = (skel.at[0, pl.ds(0, 7), pl.ds(0, FEAT)], skel.at[0, pl.ds(0, 7), pl.ds(FEAT, COLS)])

    def hand_on(slot, part_of, k):
        remote(skel.at[slot, part_of], skel.at[slot + 1, part_of], s_send.at[3, 0],
               x_recv.at[slot + 1, k], at_grp(0, 1))

    halves = (pl.ds(0, 4), pl.ds(4, 4))

    def do_own():
        for kind in (0, 1):
            whole(others[kind], s_recv.at[3, kind])
        for first in (0, 1):
            for dx in (1, 3):
                there, k = 2 * (4 - dx), first if dx == 3 else 1 - first
                remote(skel.at[0, halves[k]], skel.at[there, halves[k]], s_send.at[3, 0],
                       x_recv.at[there, k], at_grp(dx, 0))
        for k in (0, 1):
            hand_on(0, halves[k], k)

    def do_relay(dx):
        k = 0 if dx == 1 else 1
        whole(skel.at[2 * dx, halves[k]], x_recv.at[2 * dx, k])
        remote(skel.at[2 * dx, halves[k]], skel.at[4, halves[k]], s_send.at[3, 1],
               x_recv.at[4, k], at_grp(4 - dx, 0))
        hand_on(2 * dx, halves[k], k)

    def do_rest(dx):
        k = 1 if dx == 1 else 0
        whole(skel.at[2 * dx, halves[k]], x_recv.at[2 * dx, k])
        hand_on(2 * dx, halves[k], k)

    def do_last():
        for k in (0, 1):
            whole(skel.at[4, halves[k]], x_recv.at[4, k])
            hand_on(4, halves[k], k)

    def block(xs, ws):
        rhs = jnp.concatenate([xs, aug_rows(half_norm(xs), 0)], axis=0)
        arg = jnp.dot(lhs[...], rhs, preferred_element_type=F32)
        kern = jnp.exp(arg).astype(BF)
        return lax.dot_general(kern, ws, (((1,), (1,)), ((), ())), preferred_element_type=F32)

    def do_targets():
        xt = gat[0, :FEAT]
        rows = jnp.concatenate([xt, aug_rows(half_norm(xt), 1)], axis=0)
        pad = jnp.zeros((128 - rows.shape[0], PTS), F32)
        turned = jnp.concatenate([rows.astype(F32), pad], axis=0).T
        lhs[...] = turned[:, :FEAT + 16].astype(BF)

    def do_self():
        acc[...] = block(gat[0, :FEAT], gat[0, FEAT:])

    def do_far(rel):
        if rel % 2 == 1:
            for k in (0, 1):
                whole(skel.at[rel, halves[k]], x_recv.at[rel, k])
        both = jnp.concatenate([skel[rel, i] for i in range(SIDE)], axis=1)
        acc[...] += (block(both[:FEAT, :PTS], both[FEAT:, :PTS])
                     + block(both[:FEAT, PTS:], both[FEAT:, PTS:]))

    work = {"wait": do_wait, "send": do_send, "part": do_part, "sum1": do_sum1,
            "sum2": do_sum2, "sum3": do_sum3, "own": do_own, "targets": do_targets, "self": do_self}
    for dx in (1, 3):
        work["relay%d" % dx] = functools.partial(do_relay, dx)
        work["rest%d" % dx] = functools.partial(do_rest, dx)
    work["last"] = do_last
    for rel in range(1, 8):
        work["far%d" % rel] = functools.partial(do_far, rel)
    for name, *args in schedule()[0]:
        work[name](*args)

    own[4].wait()
    own[5].wait()
    mine = count_ref[leaf]

    @pl.loop(0, SLOTS // 5)
    def _(i):
        add = jnp.zeros((PTS, COLS), F32)
        for j in range(5):
            k = 1 + 5 * i + j
            source = near_ref[k, leaf]
            sy = (source // SIDE + SIDE - y) % SIDE
            sz = (source % SIDE + SIDE - z) % SIDE
            got = gat[sy * SIDE + sz]
            used = jnp.where(k < mine, 1.0, 0.0).astype(F32)
            add = add + block(got[:FEAT], (got[FEAT:].astype(F32) * used).astype(BF))
        acc[...] += add

    pad = jnp.zeros((PTS, 128 - COLS), F32)
    out_ref[...] = jnp.concatenate([acc[...], pad], axis=1).T[:COLS]

    whole(gat.at[pl.ds(0, 63)], g_send)
    for kind in (0, 1):
        whole(got1.at[kind], s_send.at[0, kind])
        by_count(kind, lambda n: (mid_p, mid_w)[kind].at[pl.ds(0, 16 * n)], s_send.at[1, kind])
        place, every, _, _ = takes[kind]

        @pl.when(place % every == 0)
        def _():
            whole(skel.at[0, 0:7, pl.ds(0, 16)], s_send.at[2, kind])

        whole(others[kind], s_send.at[4, kind])
    whole(skel.at[pl.ds(0, 6)], s_send.at[3, 0])
    whole(skel.at[0], s_send.at[3, 1])


def per_device(points, weights, interp, near_leaf, near_count, skel_index):
    flops = 2 * 30 * PTS * PTS * (FEAT + 16 + COLS) + 2 * PTS * SKEL * ROWS
    out = pl.pallas_call(
        kernel,
        out_shape=jax.ShapeDtypeStruct((COLS, PTS), F32),
        in_specs=[pl.BlockSpec(memory_space=pltpu.HBM)] * 6,
        out_specs=pl.BlockSpec(memory_space=pltpu.VMEM),
        scratch_shapes=[
            pltpu.VMEM((64, ROWS, PTS), BF),
            pltpu.VMEM((PTS, SKEL), BF),
            pltpu.SMEM((SLOTS, 64), jnp.int32),
            pltpu.SMEM((64,), jnp.int32),
            pltpu.VMEM((1, SKEL), jnp.int32),
            pltpu.VMEM((2, SIDE, FEAT, PIECE), BF),
            pltpu.VMEM((2, SIDE - 1, FEAT, PIECE), BF),
            pltpu.VMEM((FEAT, PIECE), BF),
            pltpu.VMEM((COLS, PIECE), F32),
            pltpu.VMEM((SIDE - 1, 16, PIECE), BF),
            pltpu.VMEM((SIDE - 1, 16, PIECE), F32),
            pltpu.VMEM((8, SIDE, ROWS, PIECE), BF),
            pltpu.VMEM((PTS, FEAT + 16), BF),
            pltpu.VMEM((PTS, COLS), F32),
            pltpu.SemaphoreType.DMA((6,)),
            pltpu.SemaphoreType.DMA,
            pltpu.SemaphoreType.DMA((2, 64)),
            pltpu.SemaphoreType.DMA((5, 2)),
            pltpu.SemaphoreType.DMA((4, 2)),
            pltpu.SemaphoreType.DMA((8, 2)),
        ],
        cost_estimate=pl.CostEstimate(
            flops=flops, bytes_accessed=2 * PTS * SKEL, transcendentals=30 * PTS * PTS
        ),
        compiler_params=pltpu.CompilerParams(
            collective_id=0, has_side_effects=True, vmem_limit_bytes=60 * 1024 * 1024
        ),
    )(near_leaf.T, near_count, skel_index, points.T, weights.T, interp)
    return out.T


def solution(mesh):
    placed = (
        P(("grp", "leaf"), None),
        P(("grp", "leaf"), None),
        P(("grp", "leaf"), None),
        P("grp", None),
        P("grp"),
        P("grp", None),
    )
    return jax.shard_map(
        per_device, mesh=mesh, in_specs=placed, out_specs=P(("grp", "leaf"), None), check_vma=False
    )
```

```python
import functools
import heapq

import jax
import jax.numpy as jnp
from jax import lax
from jax.experimental import pallas as pl
from jax.experimental.pallas import tpu as pltpu
from jax.sharding import PartitionSpec as P

MESH = pl.DeviceIdType.MESH
BF, F32 = jnp.bfloat16, jnp.float32
SIDE = 8
PTS, FEAT, COLS, SKEL, SLOTS = 512, 64, 32, 1024, 16
ROWS = FEAT + COLS
HALF = ROWS // 2
PIECE = SKEL // SIDE

FIRST = ((4, 3), (3, 4))


def second(o):
    return (4, 3) if o & 1 else (3, 4)


def hops(half, o1, o2):
    out = []
    if o2 == 0:
        if o1 <= 0 and -o1 < FIRST[half][0]:
            out.append((0, 1))
        if o1 >= 0 and o1 < FIRST[half][1]:
            out.append((0, -1))
        out += [(1, 1), (1, -1)]
    else:
        plus, minus = second(o1)
        if o2 < 0 and -o2 < plus:
            out.append((1, 1))
        if o2 > 0 and o2 < minus:
            out.append((1, -1))
    return out


CHUNK, HOP, LEAD, STAGE, PART = 0.98, 1.7, 2.0, 2.2, 2.2


def schedule():
    links = [(axis, sign) for axis in (0, 1) for sign in (1, -1)]
    free = {link: 0.0 for link in links}
    queue = {link: [] for link in links}
    arrivals, ready, program = [], [(0.0, 0, "part")], []
    count, now = 0, 0.0

    def left(half, o1, o2, leg, sign):
        reach = FIRST[half] if leg == 0 else second(o1)
        gone = abs(o1) if leg == 0 else abs(o2)
        return reach[0 if sign > 0 else 1] - gone + (4 if leg == 0 else 0)

    def enqueue(half, o1, o2):
        nonlocal count
        for leg, sign in hops(half, o1, o2):
            count += 1
            item = (-left(half, o1, o2, leg, sign), count, half, o1, o2, leg, sign)
            heapq.heappush(queue[((half + leg) % 2, sign)], item)

    def burst(share, after):
        nonlocal count
        end = now
        for axis, sign in links:
            free[axis, sign] = max(now, free[axis, sign]) + 8 * share[axis] * CHUNK
            end = max(end, free[axis, sign])
        count += 1
        heapq.heappush(ready, (end + STAGE, count, after))

    def at(delay, *names):
        nonlocal count
        for name in names:
            count += 1
            heapq.heappush(ready, (now + delay, count, name))

    for half in (0, 1):
        enqueue(half, 0, 0)
    while True:
        if arrivals and arrivals[0][0] <= now:
            _, _, half, o1, o2 = heapq.heappop(arrivals)
            program.append(("wait", half, o1, o2))
            now += 0.04
            enqueue(half, o1, o2)
            continue
        open_links = [k for k in links if queue[k] and free[k] - now <= LEAD]
        if open_links:
            link = min(open_links, key=lambda k: free[k])
            _, _, half, o1, o2, leg, sign = heapq.heappop(queue[link])
            program.append(("send", half, o1, o2, leg, sign))
            free[link] = max(now, free[link]) + CHUNK
            seen = (o1 - sign, o2) if leg == 0 else (o1, o2 - sign)
            count += 1
            heapq.heappush(arrivals, (free[link] + HOP, count, half) + seen)
            now += 0.03
            continue
        if ready and ready[0][0] <= now:
            name = heapq.heappop(ready)[2]
            program.append((name,))
            if name == "part":
                now += PART
                burst((1 / 3, 1 / 3), "sum1")
                at(0.0, "targets")
            elif name == "targets":
                now += 0.6
                at(0.0, "self")
            elif name == "sum1":
                now += 0.3
                burst((1 / 24, 1 / 24), "sum2")
            elif name == "sum2":
                now += 0.2
                burst((1 / 24, 1 / 48), "sum3")
            elif name == "sum3":
                burst((1 / 6, 1 / 3), "own")
            elif name == "own":
                at(3.0, "far1")
                at(4.2, "relay1", "relay3")
                at(6.2, "rest1", "rest3")
                at(8.6, "last")
            elif name in ("rest1", "rest3"):
                at(0.2, "far" + {"rest1": "2", "rest3": "6"}[name])
                at(2.5, "far" + {"rest1": "3", "rest3": "7"}[name])
            elif name == "last":
                at(0.2, "far4")
                at(2.5, "far5")
            elif name in ("relay1", "relay3"):
                pass
            else:
                now += 0.36 if name == "self" else 0.72
            continue
        times = [free[k] - LEAD for k in links if queue[k]]
        times += [arrivals[0][0]] if arrivals else []
        times += [ready[0][0]] if ready else []
        if not times:
            return program, now
        now = max(now + 1e-3, min(times))


def slot_of(half, o1, o2):
    oz, oy = (o1, o2) if half == 0 else (o2, o1)
    return (oy % SIDE) * SIDE + oz % SIDE


def split3(v):
    hi = v.astype(BF).astype(F32)
    mid = (v - hi).astype(BF).astype(F32)
    return hi, mid, v - hi - mid


def aug_rows(v, first):
    hi, mid, lo = split3(v)
    row = lax.broadcasted_iota(jnp.int32, (16, v.shape[1]), 0)
    k = row - 3 * first
    terms = jnp.where(k == 0, hi, jnp.where(k == 1, mid, lo))
    mine = (k >= 0) & (k < 3)
    return jnp.where(mine, terms, jnp.where(row < 6, 1.0, 0.0)).astype(BF)


def half_norm(xt):
    xf = xt.astype(F32)
    return -0.5 * jnp.sum(xf * xf, axis=0, keepdims=True)


def kernel(
    near_hbm, count_hbm, index_hbm, pts_ref, wts_ref, interp_ref, out_ref,
    gat, interp_v, near_ref, count_ref, index_v, part, got1, mid_p, mid_w, got_p, got_w, skel, lhs, acc,
    loc, g_send, g_recv, s_send, s_recv, x_recv,
):
    grp, leaf = lax.axis_index("grp"), lax.axis_index("leaf")
    x, core = grp // 2, grp % 2
    y, z = leaf // SIDE, leaf % SIDE

    def at_leaf(oy, oz):
        return (grp, ((y + oy + SIDE) % SIDE) * SIDE + (z + oz + SIDE) % SIDE)

    def at_grp(ox, oc):
        return (((x + ox) % 4) * 2 + (core + oc) % 2, leaf)

    barrier = pltpu.get_barrier_semaphore()
    peers = [at_leaf(0, o) for o in range(1, SIDE)] + [at_leaf(o, 0) for o in range(1, SIDE)]
    peers += [at_grp(1, 0), at_grp(3, 0), at_grp(0, 1)]
    for peer in peers:
        pl.semaphore_signal(barrier, inc=1, device_id=peer, device_id_type=MESH)
    own = [
        pltpu.make_async_copy(pts_ref, gat.at[0, pl.ds(0, FEAT)], loc.at[0]),
        pltpu.make_async_copy(wts_ref, gat.at[0, pl.ds(FEAT, COLS)], loc.at[1]),
        pltpu.make_async_copy(interp_ref, interp_v, loc.at[2]),
        pltpu.make_async_copy(index_hbm, index_v, loc.at[3]),
        pltpu.make_async_copy(near_hbm, near_ref, loc.at[4]),
        pltpu.make_async_copy(count_hbm, count_ref, loc.at[5]),
    ]
    for c in own:
        c.start()
    pl.semaphore_wait(barrier, len(peers))

    def remote(src, dst, send, recv, peer):
        pltpu.make_async_remote_copy(
            src_ref=src, dst_ref=dst, send_sem=send, recv_sem=recv,
            device_id=peer, device_id_type=MESH,
        ).start()

    def whole(ref, sem):
        pltpu.make_async_copy(ref, ref, sem).wait()

    def do_send(half, o1, o2, leg, sign):
        here = slot_of(half, o1, o2)
        there = slot_of(half, *((o1 - sign, o2) if leg == 0 else (o1, o2 - sign)))
        rows = pl.ds(half * HALF, HALF)
        peer = at_leaf(0, sign) if (half + leg) % 2 == 0 else at_leaf(sign, 0)
        parts = [(gat.at[here, rows], rows)]
        if here == 0 and half == 0:
            parts = [(pts_ref.at[rows], rows)]
        elif here == 0:
            last, below = pl.ds(HALF, FEAT - HALF), pl.ds(FEAT, COLS)
            parts = [(pts_ref.at[last], last), (wts_ref, below)]
        for src, place in parts:
            remote(src, gat.at[there, place], g_send, g_recv.at[half, there], peer)

    def do_wait(half, o1, o2):
        here = slot_of(half, o1, o2)
        whole(gat.at[here, pl.ds(half * HALF, HALF)], g_recv.at[half, here])

    def do_part():
        for c in own[:4]:
            c.wait()
        index = index_v[...] - leaf * PTS
        pick = lax.broadcasted_iota(jnp.int32, (PTS, SKEL), 0) == index
        pts = jnp.dot(gat[0, :FEAT], pick.astype(BF), preferred_element_type=F32).astype(BF)
        wts = jnp.dot(gat[0, FEAT:], interp_v[...], preferred_element_type=F32)
        hi = wts.astype(BF)
        lo = (wts - hi.astype(F32)).astype(BF)
        for k in range(SIDE):
            cols = slice(k * PIECE, (k + 1) * PIECE)
            part[0, k] = pts[:, cols]
            part[1, k, :COLS] = hi[:, cols]
            part[1, k, COLS:] = lo[:, cols]
        for o in range(1, SIDE):
            for kind, place in ((0, y), (1, z)):
                remote(part.at[kind, (place + o) % SIDE], got1.at[kind, 7 - o], s_send.at[0, kind],
                       s_recv.at[0, kind], peer_on(1 - kind, o))

    takes = ((z, 2, y, FEAT // 16), (y, 4, z, COLS // 16))

    def peer_on(kind, o):
        return at_leaf(0, o) if kind == 0 else at_leaf(o, 0)

    def total(kind, first, got):
        v = first.astype(F32)
        for k in range(SIDE - 1):
            v = v + got[kind, k].astype(F32)
        return v if kind == 0 else v[:COLS] + v[COLS:]

    def do_sum1():
        for kind in (0, 1):
            whole(got1.at[kind], s_recv.at[0, kind])
        mid_p[...] = total(0, part[0, y], got1).astype(BF)
        mid_w[...] = total(1, part[1, z], got1)
        for kind, (mid, got) in enumerate(((mid_p, got_p), (mid_w, got_w))):
            place, every, _, chunks = takes[kind]
            for c in range(chunks):
                off = (every * c - place + SIDE) % SIDE

                @pl.when(off != 0)
                def _():
                    remote(mid.at[pl.ds(16 * c, 16)], got.at[SIDE - 1 - off], s_send.at[1, kind],
                           s_recv.at[1, kind], peer_on(kind, off))

    def do_sum2():
        for kind, (mid, got) in enumerate(((mid_p, got_p), (mid_w, got_w))):
            place, every, piece, _ = takes[kind]

            @pl.when(place % every == 0)
            def _():
                whole(got, s_recv.at[1, kind])
                row = pl.multiple_of(place // every * 16, 16)
                v = mid[pl.ds(row, 16)].astype(F32)
                for k in range(SIDE - 1):
                    v = v + got[k].astype(F32)
                mine = pl.ds(pl.multiple_of(kind * FEAT + row, 16), 16)
                skel[0, piece, mine] = v.astype(BF)
                for o in range(1, SIDE):
                    ref = skel.at[0, piece, mine]
                    remote(ref, ref, s_send.at[2, kind], s_recv.at[2, kind], peer_on(kind, o))

    def by_count(kind, one, sem):
        place, every, _, chunks = takes[kind]
        for here in (0, 1):
            @pl.when((place % every == 0) if here else (place % every != 0))
            def _():
                whole(one(chunks - here), sem)

    def do_sum3():
        for kind in (0, 1):
            by_count(kind, lambda n: skel.at[0, 0, pl.ds(0, 16 * n)], s_recv.at[2, kind])
        p, w = skel.at[0, y, pl.ds(0, FEAT)], skel.at[0, z, pl.ds(FEAT, COLS)]
        for o in range(1, SIDE):
            remote(p, p, s_send.at[4, 0], s_recv.at[3, 0], at_leaf(o, 0))
            remote(w, w, s_send.at[4, 1], s_recv.at[3, 1], at_leaf(0, o))

    others = (skel.at[0, pl.ds(0, 7), pl.ds(0, FEAT)], skel.at[0, pl.ds(0, 7), pl.ds(FEAT, COLS)])

    def hand_on(slot, part_of, k):
        remote(skel.at[slot, part_of], skel.at[slot + 1, part_of], s_send.at[3, 0],
               x_recv.at[slot + 1, k], at_grp(0, 1))

    halves = (pl.ds(0, 4), pl.ds(4, 4))

    def do_own():
        for kind in (0, 1):
            whole(others[kind], s_recv.at[3, kind])
        for first in (0, 1):
            for dx in (1, 3):
                there, k = 2 * (4 - dx), first if dx == 3 else 1 - first
                remote(skel.at[0, halves[k]], skel.at[there, halves[k]], s_send.at[3, 0],
                       x_recv.at[there, k], at_grp(dx, 0))
        for k in (0, 1):
            hand_on(0, halves[k], k)

    def do_relay(dx):
        k = 0 if dx == 1 else 1
        whole(skel.at[2 * dx, halves[k]], x_recv.at[2 * dx, k])
        remote(skel.at[2 * dx, halves[k]], skel.at[4, halves[k]], s_send.at[3, 1],
               x_recv.at[4, k], at_grp(4 - dx, 0))
        hand_on(2 * dx, halves[k], k)

    def do_rest(dx):
        k = 1 if dx == 1 else 0
        whole(skel.at[2 * dx, halves[k]], x_recv.at[2 * dx, k])
        hand_on(2 * dx, halves[k], k)

    def do_last():
        for k in (0, 1):
            whole(skel.at[4, halves[k]], x_recv.at[4, k])
            hand_on(4, halves[k], k)

    def block(xs, ws):
        rhs = jnp.concatenate([xs, aug_rows(half_norm(xs), 0)], axis=0)
        arg = jnp.dot(lhs[...], rhs, preferred_element_type=F32)
        kern = jnp.exp(arg).astype(BF)
        return lax.dot_general(kern, ws, (((1,), (1,)), ((), ())), preferred_element_type=F32)

    def do_targets():
        xt = gat[0, :FEAT]
        rows = jnp.concatenate([xt, aug_rows(half_norm(xt), 1)], axis=0)
        pad = jnp.zeros((128 - rows.shape[0], PTS), F32)
        turned = jnp.concatenate([rows.astype(F32), pad], axis=0).T
        lhs[...] = turned[:, :FEAT + 16].astype(BF)

    def do_self():
        acc[...] = block(gat[0, :FEAT], gat[0, FEAT:])

    def do_far(rel):
        if rel % 2 == 1:
            for k in (0, 1):
                whole(skel.at[rel, halves[k]], x_recv.at[rel, k])
        both = jnp.concatenate([skel[rel, i] for i in range(SIDE)], axis=1)
        acc[...] += (block(both[:FEAT, :PTS], both[FEAT:, :PTS])
                     + block(both[:FEAT, PTS:], both[FEAT:, PTS:]))

    work = {"wait": do_wait, "send": do_send, "part": do_part, "sum1": do_sum1,
            "sum2": do_sum2, "sum3": do_sum3, "own": do_own, "targets": do_targets, "self": do_self}
    for dx in (1, 3):
        work["relay%d" % dx] = functools.partial(do_relay, dx)
        work["rest%d" % dx] = functools.partial(do_rest, dx)
    work["last"] = do_last
    for rel in range(1, 8):
        work["far%d" % rel] = functools.partial(do_far, rel)
    for name, *args in schedule()[0]:
        work[name](*args)

    own[4].wait()
    own[5].wait()
    mine = count_ref[leaf]

    add = jnp.zeros((PTS, COLS), F32)
    for k in range(1, SLOTS):
        source = near_ref[k, leaf]
        sy = (source // SIDE + SIDE - y) % SIDE
        sz = (source % SIDE + SIDE - z) % SIDE
        got = gat[sy * SIDE + sz]
        used = jnp.where(k < mine, 1.0, 0.0).astype(F32)
        add = add + block(got[:FEAT], (got[FEAT:].astype(F32) * used).astype(BF))
    acc[...] += add

    pad = jnp.zeros((PTS, 128 - COLS), F32)
    out_ref[...] = jnp.concatenate([acc[...], pad], axis=1).T[:COLS]

    whole(gat.at[pl.ds(0, 63)], g_send)
    for kind in (0, 1):
        whole(got1.at[kind], s_send.at[0, kind])
        by_count(kind, lambda n: (mid_p, mid_w)[kind].at[pl.ds(0, 16 * n)], s_send.at[1, kind])
        place, every, _, _ = takes[kind]

        @pl.when(place % every == 0)
        def _():
            whole(skel.at[0, 0:7, pl.ds(0, 16)], s_send.at[2, kind])

        whole(others[kind], s_send.at[4, kind])
    whole(skel.at[pl.ds(0, 6)], s_send.at[3, 0])
    whole(skel.at[0], s_send.at[3, 1])


def per_device(points, weights, interp, near_leaf, near_count, skel_index):
    flops = 2 * 30 * PTS * PTS * (FEAT + 16 + COLS) + 2 * PTS * SKEL * ROWS
    given = (near_leaf.T, near_count, skel_index, points.T, weights.T, interp)
    out = pl.pallas_call(
        kernel,
        out_shape=jax.ShapeDtypeStruct((COLS, PTS), F32),
        in_specs=[pl.BlockSpec(memory_space=pltpu.HBM)] * 6,
        out_specs=pl.BlockSpec(memory_space=pltpu.VMEM),
        scratch_shapes=[
            pltpu.VMEM((64, ROWS, PTS), BF),
            pltpu.VMEM((PTS, SKEL), BF),
            pltpu.SMEM((SLOTS, 64), jnp.int32),
            pltpu.SMEM((64,), jnp.int32),
            pltpu.VMEM((1, SKEL), jnp.int32),
            pltpu.VMEM((2, SIDE, FEAT, PIECE), BF),
            pltpu.VMEM((2, SIDE - 1, FEAT, PIECE), BF),
            pltpu.VMEM((FEAT, PIECE), BF),
            pltpu.VMEM((COLS, PIECE), F32),
            pltpu.VMEM((SIDE - 1, 16, PIECE), BF),
            pltpu.VMEM((SIDE - 1, 16, PIECE), F32),
            pltpu.VMEM((8, SIDE, ROWS, PIECE), BF),
            pltpu.VMEM((PTS, FEAT + 16), BF),
            pltpu.VMEM((PTS, COLS), F32),
            pltpu.SemaphoreType.DMA((6,)),
            pltpu.SemaphoreType.DMA,
            pltpu.SemaphoreType.DMA((2, 64)),
            pltpu.SemaphoreType.DMA((5, 2)),
            pltpu.SemaphoreType.DMA((4, 2)),
            pltpu.SemaphoreType.DMA((8, 2)),
        ],
        cost_estimate=pl.CostEstimate(
            flops=flops, bytes_accessed=2 * PTS * SKEL, transcendentals=30 * PTS * PTS
        ),
        compiler_params=pltpu.CompilerParams(
            collective_id=0, has_side_effects=True, vmem_limit_bytes=40 * 1024 * 1024
        ),
    )(*[pltpu.with_memory_space_constraint(a, pltpu.HBM) for a in given])
    return out.T


def solution(mesh):
    placed = (
        P(("grp", "leaf"), None),
        P(("grp", "leaf"), None),
        P(("grp", "leaf"), None),
        P("grp", None),
        P("grp"),
        P("grp", None),
    )
    return jax.shard_map(
        per_device, mesh=mesh, in_specs=placed, out_specs=P(("grp", "leaf"), None), check_vma=False
    )
```

```python
import functools
import heapq

import jax
import jax.numpy as jnp
from jax import lax
from jax.experimental import pallas as pl
from jax.experimental.pallas import tpu as pltpu
from jax.sharding import PartitionSpec as P

MESH = pl.DeviceIdType.MESH
BF, F32 = jnp.bfloat16, jnp.float32
SIDE = 8
PTS, FEAT, COLS, SKEL, SLOTS = 512, 64, 32, 1024, 16
ROWS = FEAT + COLS
HALF = ROWS // 2
PIECE = SKEL // SIDE
FARTHEST = (4, 3, 5, 2, 6, 1, 7)

FIRST = ((4, 3), (3, 4))


def second(o):
    return (4, 3) if o & 1 else (3, 4)


def hops(half, o1, o2):
    out = []
    if o2 == 0:
        if o1 <= 0 and -o1 < FIRST[half][0]:
            out.append((0, 1))
        if o1 >= 0 and o1 < FIRST[half][1]:
            out.append((0, -1))
        out += [(1, 1), (1, -1)]
    else:
        plus, minus = second(o1)
        if o2 < 0 and -o2 < plus:
            out.append((1, 1))
        if o2 > 0 and o2 < minus:
            out.append((1, -1))
    return out


CHUNK, HOP, LEAD, STAGE, PART = 0.98, 1.7, 2.0, 2.2, 2.2


def schedule():
    links = [(axis, sign) for axis in (0, 1) for sign in (1, -1)]
    free = {link: 0.0 for link in links}
    queue = {link: [] for link in links}
    arrivals, ready, program = [], [(0.0, 0, "part")], []
    count, now = 0, 0.0

    def left(half, o1, o2, leg, sign):
        reach = FIRST[half] if leg == 0 else second(o1)
        gone = abs(o1) if leg == 0 else abs(o2)
        return reach[0 if sign > 0 else 1] - gone + (4 if leg == 0 else 0)

    def enqueue(half, o1, o2):
        nonlocal count
        for leg, sign in hops(half, o1, o2):
            count += 1
            item = (-left(half, o1, o2, leg, sign), count, half, o1, o2, leg, sign)
            heapq.heappush(queue[((half + leg) % 2, sign)], item)

    def burst(share, after):
        nonlocal count
        end = now
        for axis, sign in links:
            free[axis, sign] = max(now, free[axis, sign]) + 8 * share[axis] * CHUNK
            end = max(end, free[axis, sign])
        count += 1
        heapq.heappush(ready, (end + STAGE, count, after))

    def at(delay, *names):
        nonlocal count
        for name in names:
            count += 1
            heapq.heappush(ready, (now + delay, count, name))

    for half in (0, 1):
        enqueue(half, 0, 0)
    while True:
        if arrivals and arrivals[0][0] <= now:
            _, _, half, o1, o2 = heapq.heappop(arrivals)
            program.append(("wait", half, o1, o2))
            now += 0.04
            enqueue(half, o1, o2)
            continue
        open_links = [k for k in links if queue[k] and free[k] - now <= LEAD]
        if open_links:
            link = min(open_links, key=lambda k: free[k])
            _, _, half, o1, o2, leg, sign = heapq.heappop(queue[link])
            program.append(("send", half, o1, o2, leg, sign))
            free[link] = max(now, free[link]) + CHUNK
            seen = (o1 - sign, o2) if leg == 0 else (o1, o2 - sign)
            count += 1
            heapq.heappush(arrivals, (free[link] + HOP, count, half) + seen)
            now += 0.03
            continue
        if ready and ready[0][0] <= now:
            name = heapq.heappop(ready)[2]
            program.append((name,))
            if name == "part":
                now += PART
                burst((1 / 3, 1 / 3), "sum1")
                at(0.0, "targets")
            elif name == "targets":
                now += 0.6
                at(0.0, "self")
            elif name == "sum1":
                now += 0.3
                burst((1 / 24, 1 / 24), "sum2")
            elif name == "sum2":
                now += 0.2
                burst((1 / 24, 1 / 48), "sum3")
            elif name == "sum3":
                burst((1 / 6, 1 / 3), "own")
            elif name == "own":
                at(3.0, "far1")
                at(4.2, "relay1", "relay3")
                at(6.2, "rest1", "rest3")
                at(8.6, "last")
            elif name in ("rest1", "rest3"):
                at(0.2, "far" + {"rest1": "2", "rest3": "6"}[name])
                at(2.5, "far" + {"rest1": "3", "rest3": "7"}[name])
            elif name == "last":
                at(0.2, "far4")
                at(2.5, "far5")
            elif name in ("relay1", "relay3"):
                pass
            else:
                now += 0.36 if name == "self" else 0.72
            continue
        times = [free[k] - LEAD for k in links if queue[k]]
        times += [arrivals[0][0]] if arrivals else []
        times += [ready[0][0]] if ready else []
        if not times:
            return program, now
        now = max(now + 1e-3, min(times))


def slot_of(half, o1, o2):
    oz, oy = (o1, o2) if half == 0 else (o2, o1)
    return (oy % SIDE) * SIDE + oz % SIDE


def split3(v):
    hi = v.astype(BF).astype(F32)
    mid = (v - hi).astype(BF).astype(F32)
    return hi, mid, v - hi - mid


def aug_rows(v, first):
    hi, mid, lo = split3(v)
    row = lax.broadcasted_iota(jnp.int32, (16, v.shape[1]), 0)
    k = row - 3 * first
    terms = jnp.where(k == 0, hi, jnp.where(k == 1, mid, lo))
    mine = (k >= 0) & (k < 3)
    return jnp.where(mine, terms, jnp.where(row < 6, 1.0, 0.0)).astype(BF)


def half_norm(xt):
    xf = xt.astype(F32)
    return -0.5 * jnp.sum(xf * xf, axis=0, keepdims=True)


def kernel(
    near_hbm, count_hbm, index_hbm, pts_ref, wts_ref, interp_ref, out_ref,
    gat, interp_v, near_ref, count_ref, index_v, part, got1, mid_p, mid_w, got_p, got_w, skel, lhs, acc,
    loc, g_send, g_recv, s_send, s_recv, x_recv,
):
    grp, leaf = lax.axis_index("grp"), lax.axis_index("leaf")
    x, core = grp // 2, grp % 2
    y, z = leaf // SIDE, leaf % SIDE

    def at_leaf(oy, oz):
        return (grp, ((y + oy + SIDE) % SIDE) * SIDE + (z + oz + SIDE) % SIDE)

    def at_grp(ox, oc):
        return (((x + ox) % 4) * 2 + (core + oc) % 2, leaf)

    barrier = pltpu.get_barrier_semaphore()
    peers = [at_leaf(0, o) for o in range(1, SIDE)] + [at_leaf(o, 0) for o in range(1, SIDE)]
    peers += [at_grp(1, 0), at_grp(3, 0), at_grp(0, 1)]
    for peer in peers:
        pl.semaphore_signal(barrier, inc=1, device_id=peer, device_id_type=MESH)
    own = [
        pltpu.make_async_copy(pts_ref, gat.at[0, pl.ds(0, FEAT)], loc.at[0]),
        pltpu.make_async_copy(wts_ref, gat.at[0, pl.ds(FEAT, COLS)], loc.at[1]),
        pltpu.make_async_copy(interp_ref, interp_v, loc.at[2]),
        pltpu.make_async_copy(index_hbm, index_v, loc.at[3]),
        pltpu.make_async_copy(near_hbm, near_ref, loc.at[4]),
        pltpu.make_async_copy(count_hbm, count_ref, loc.at[5]),
    ]
    for c in own:
        c.start()
    pl.semaphore_wait(barrier, len(peers))

    def remote(src, dst, send, recv, peer):
        pltpu.make_async_remote_copy(
            src_ref=src, dst_ref=dst, send_sem=send, recv_sem=recv,
            device_id=peer, device_id_type=MESH,
        ).start()

    def whole(ref, sem):
        pltpu.make_async_copy(ref, ref, sem).wait()

    def do_send(half, o1, o2, leg, sign):
        here = slot_of(half, o1, o2)
        there = slot_of(half, *((o1 - sign, o2) if leg == 0 else (o1, o2 - sign)))
        rows = pl.ds(half * HALF, HALF)
        peer = at_leaf(0, sign) if (half + leg) % 2 == 0 else at_leaf(sign, 0)
        parts = [(gat.at[here, rows], rows)]
        if here == 0 and half == 0:
            parts = [(pts_ref.at[rows], rows)]
        elif here == 0:
            last, below = pl.ds(HALF, FEAT - HALF), pl.ds(FEAT, COLS)
            parts = [(pts_ref.at[last], last), (wts_ref, below)]
        for src, place in parts:
            remote(src, gat.at[there, place], g_send, g_recv.at[half, there], peer)

    def do_wait(half, o1, o2):
        here = slot_of(half, o1, o2)
        whole(gat.at[here, pl.ds(half * HALF, HALF)], g_recv.at[half, here])

    def scatter(kind, place):
        for o in FARTHEST:
            remote(part.at[kind, (place + o) % SIDE], got1.at[kind, 7 - o], s_send.at[0, kind],
                   s_recv.at[0, kind], peer_on(1 - kind, o))

    def do_part():
        for c in own[:4]:
            c.wait()
        index = index_v[...] - leaf * PTS
        pick = lax.broadcasted_iota(jnp.int32, (PTS, SKEL), 0) == index
        pts = jnp.dot(gat[0, :FEAT], pick.astype(BF), preferred_element_type=F32).astype(BF)
        for k in range(SIDE):
            part[0, k] = pts[:, k * PIECE:(k + 1) * PIECE]
        scatter(0, y)
        wts = jnp.dot(gat[0, FEAT:], interp_v[...], preferred_element_type=F32)
        hi = wts.astype(BF)
        lo = (wts - hi.astype(F32)).astype(BF)
        for k in range(SIDE):
            cols = slice(k * PIECE, (k + 1) * PIECE)
            part[1, k, :COLS] = hi[:, cols]
            part[1, k, COLS:] = lo[:, cols]
        scatter(1, z)

    takes = ((z, 2, y, FEAT // 16), (y, 4, z, COLS // 16))

    def peer_on(kind, o):
        return at_leaf(0, o) if kind == 0 else at_leaf(o, 0)

    def total(kind, first, got):
        v = first.astype(F32)
        for k in range(SIDE - 1):
            v = v + got[kind, k].astype(F32)
        return v if kind == 0 else v[:COLS] + v[COLS:]

    def do_sum1():
        for kind in (0, 1):
            whole(got1.at[kind], s_recv.at[0, kind])
        mid_p[...] = total(0, part[0, y], got1).astype(BF)
        mid_w[...] = total(1, part[1, z], got1)
        for kind, (mid, got) in enumerate(((mid_p, got_p), (mid_w, got_w))):
            place, every, _, chunks = takes[kind]
            for c in range(chunks):
                off = (every * c - place + SIDE) % SIDE

                @pl.when(off != 0)
                def _():
                    remote(mid.at[pl.ds(16 * c, 16)], got.at[SIDE - 1 - off], s_send.at[1, kind],
                           s_recv.at[1, kind], peer_on(kind, off))

    def do_sum2():
        for kind, (mid, got) in enumerate(((mid_p, got_p), (mid_w, got_w))):
            place, every, piece, _ = takes[kind]

            @pl.when(place % every == 0)
            def _():
                whole(got, s_recv.at[1, kind])
                row = pl.multiple_of(place // every * 16, 16)
                v = mid[pl.ds(row, 16)].astype(F32)
                for k in range(SIDE - 1):
                    v = v + got[k].astype(F32)
                mine = pl.ds(pl.multiple_of(kind * FEAT + row, 16), 16)
                skel[0, piece, mine] = v.astype(BF)
                for o in FARTHEST:
                    ref = skel.at[0, piece, mine]
                    remote(ref, ref, s_send.at[2, kind], s_recv.at[2, kind], peer_on(kind, o))

    def by_count(kind, one, sem):
        place, every, _, chunks = takes[kind]
        for here in (0, 1):
            @pl.when((place % every == 0) if here else (place % every != 0))
            def _():
                whole(one(chunks - here), sem)

    def do_sum3():
        for kind in (0, 1):
            by_count(kind, lambda n: skel.at[0, 0, pl.ds(0, 16 * n)], s_recv.at[2, kind])
        p, w = skel.at[0, y, pl.ds(0, FEAT)], skel.at[0, z, pl.ds(FEAT, COLS)]
        for o in FARTHEST:
            remote(p, p, s_send.at[4, 0], s_recv.at[3, 0], at_leaf(o, 0))
            remote(w, w, s_send.at[4, 1], s_recv.at[3, 1], at_leaf(0, o))

    others = (skel.at[0, pl.ds(0, 7), pl.ds(0, FEAT)], skel.at[0, pl.ds(0, 7), pl.ds(FEAT, COLS)])

    def hand_on(slot, part_of, k):
        remote(skel.at[slot, part_of], skel.at[slot + 1, part_of], s_send.at[3, 0],
               x_recv.at[slot + 1, k], at_grp(0, 1))

    halves = (pl.ds(0, 4), pl.ds(4, 4))

    def do_own():
        for kind in (0, 1):
            whole(others[kind], s_recv.at[3, kind])
        for first in (0, 1):
            for dx in (1, 3):
                there, k = 2 * (4 - dx), first if dx == 3 else 1 - first
                remote(skel.at[0, halves[k]], skel.at[there, halves[k]], s_send.at[3, 0],
                       x_recv.at[there, k], at_grp(dx, 0))
        for k in (0, 1):
            hand_on(0, halves[k], k)

    def do_relay(dx):
        k = 0 if dx == 1 else 1
        whole(skel.at[2 * dx, halves[k]], x_recv.at[2 * dx, k])
        remote(skel.at[2 * dx, halves[k]], skel.at[4, halves[k]], s_send.at[3, 1],
               x_recv.at[4, k], at_grp(4 - dx, 0))
        hand_on(2 * dx, halves[k], k)

    def do_rest(dx):
        k = 1 if dx == 1 else 0
        whole(skel.at[2 * dx, halves[k]], x_recv.at[2 * dx, k])
        hand_on(2 * dx, halves[k], k)

    def do_last():
        for k in (0, 1):
            whole(skel.at[4, halves[k]], x_recv.at[4, k])
            hand_on(4, halves[k], k)

    def block(xs, ws):
        rhs = jnp.concatenate([xs, aug_rows(half_norm(xs), 0)], axis=0)
        arg = jnp.dot(lhs[...], rhs, preferred_element_type=F32)
        kern = jnp.exp(arg).astype(BF)
        return lax.dot_general(kern, ws, (((1,), (1,)), ((), ())), preferred_element_type=F32)

    def do_targets():
        xt = gat[0, :FEAT]
        rows = jnp.concatenate([xt, aug_rows(half_norm(xt), 1)], axis=0)
        pad = jnp.zeros((128 - rows.shape[0], PTS), F32)
        turned = jnp.concatenate([rows.astype(F32), pad], axis=0).T
        lhs[...] = turned[:, :FEAT + 16].astype(BF)

    def do_self():
        acc[...] = block(gat[0, :FEAT], gat[0, FEAT:])

    def do_far(rel):
        if rel % 2 == 1:
            for k in (0, 1):
                whole(skel.at[rel, halves[k]], x_recv.at[rel, k])
        both = jnp.concatenate([skel[rel, i] for i in range(SIDE)], axis=1)
        acc[...] += (block(both[:FEAT, :PTS], both[FEAT:, :PTS])
                     + block(both[:FEAT, PTS:], both[FEAT:, PTS:]))

    work = {"wait": do_wait, "send": do_send, "part": do_part, "sum1": do_sum1,
            "sum2": do_sum2, "sum3": do_sum3, "own": do_own, "targets": do_targets, "self": do_self}
    for dx in (1, 3):
        work["relay%d" % dx] = functools.partial(do_relay, dx)
        work["rest%d" % dx] = functools.partial(do_rest, dx)
    work["last"] = do_last
    for rel in range(1, 8):
        work["far%d" % rel] = functools.partial(do_far, rel)
    for name, *args in schedule()[0]:
        work[name](*args)

    own[4].wait()
    own[5].wait()
    mine = count_ref[leaf]

    add = jnp.zeros((PTS, COLS), F32)
    for k in range(1, SLOTS):
        source = near_ref[k, leaf]
        sy = (source // SIDE + SIDE - y) % SIDE
        sz = (source % SIDE + SIDE - z) % SIDE
        got = gat[sy * SIDE + sz]
        used = jnp.where(k < mine, 1.0, 0.0).astype(F32)
        add = add + block(got[:FEAT], (got[FEAT:].astype(F32) * used).astype(BF))
    acc[...] += add

    pad = jnp.zeros((PTS, 128 - COLS), F32)
    out_ref[...] = jnp.concatenate([acc[...], pad], axis=1).T[:COLS]

    whole(gat.at[pl.ds(0, 63)], g_send)
    for kind in (0, 1):
        whole(got1.at[kind], s_send.at[0, kind])
        by_count(kind, lambda n: (mid_p, mid_w)[kind].at[pl.ds(0, 16 * n)], s_send.at[1, kind])
        place, every, _, _ = takes[kind]

        @pl.when(place % every == 0)
        def _():
            whole(skel.at[0, 0:7, pl.ds(0, 16)], s_send.at[2, kind])

        whole(others[kind], s_send.at[4, kind])
    whole(skel.at[pl.ds(0, 6)], s_send.at[3, 0])
    whole(skel.at[0], s_send.at[3, 1])


def per_device(points, weights, interp, near_leaf, near_count, skel_index):
    flops = 2 * 30 * PTS * PTS * (FEAT + 16 + COLS) + 2 * PTS * SKEL * ROWS
    given = (near_leaf.T, near_count, skel_index, points.T, weights.T, interp)
    out = pl.pallas_call(
        kernel,
        out_shape=jax.ShapeDtypeStruct((COLS, PTS), F32),
        in_specs=[pl.BlockSpec(memory_space=pltpu.HBM)] * 6,
        out_specs=pl.BlockSpec(memory_space=pltpu.VMEM),
        scratch_shapes=[
            pltpu.VMEM((64, ROWS, PTS), BF),
            pltpu.VMEM((PTS, SKEL), BF),
            pltpu.SMEM((SLOTS, 64), jnp.int32),
            pltpu.SMEM((64,), jnp.int32),
            pltpu.VMEM((1, SKEL), jnp.int32),
            pltpu.VMEM((2, SIDE, FEAT, PIECE), BF),
            pltpu.VMEM((2, SIDE - 1, FEAT, PIECE), BF),
            pltpu.VMEM((FEAT, PIECE), BF),
            pltpu.VMEM((COLS, PIECE), F32),
            pltpu.VMEM((SIDE - 1, 16, PIECE), BF),
            pltpu.VMEM((SIDE - 1, 16, PIECE), F32),
            pltpu.VMEM((8, SIDE, ROWS, PIECE), BF),
            pltpu.VMEM((PTS, FEAT + 16), BF),
            pltpu.VMEM((PTS, COLS), F32),
            pltpu.SemaphoreType.DMA((6,)),
            pltpu.SemaphoreType.DMA,
            pltpu.SemaphoreType.DMA((2, 64)),
            pltpu.SemaphoreType.DMA((5, 2)),
            pltpu.SemaphoreType.DMA((4, 2)),
            pltpu.SemaphoreType.DMA((8, 2)),
        ],
        cost_estimate=pl.CostEstimate(
            flops=flops, bytes_accessed=2 * PTS * SKEL, transcendentals=30 * PTS * PTS
        ),
        compiler_params=pltpu.CompilerParams(
            collective_id=0, has_side_effects=True, vmem_limit_bytes=40 * 1024 * 1024
        ),
    )(*[pltpu.with_memory_space_constraint(a, pltpu.HBM) for a in given])
    return out.T


def solution(mesh):
    placed = (
        P(("grp", "leaf"), None),
        P(("grp", "leaf"), None),
        P(("grp", "leaf"), None),
        P("grp", None),
        P("grp"),
        P("grp", None),
    )
    return jax.shard_map(
        per_device, mesh=mesh, in_specs=placed, out_specs=P(("grp", "leaf"), None), check_vma=False
    )
```

```python
import functools
import heapq

import jax
import jax.numpy as jnp
from jax import lax
from jax.experimental import pallas as pl
from jax.experimental.pallas import tpu as pltpu
from jax.sharding import PartitionSpec as P

MESH = pl.DeviceIdType.MESH
BF, F32 = jnp.bfloat16, jnp.float32
SIDE = 8
PTS, FEAT, COLS, SKEL, SLOTS = 512, 64, 32, 1024, 16
ROWS = FEAT + COLS
HALF = ROWS // 2
PIECE = SKEL // SIDE
FARTHEST = (4, 3, 5, 2, 6, 1, 7)

FIRST = ((3, 4), (4, 3))


def second(o):
    return (4, 3) if o & 1 else (3, 4)


def hops(half, o1, o2):
    out = []
    if o2 == 0:
        if o1 <= 0 and -o1 < FIRST[half][0]:
            out.append((0, 1))
        if o1 >= 0 and o1 < FIRST[half][1]:
            out.append((0, -1))
        out += [(1, 1), (1, -1)]
    else:
        plus, minus = second(o1)
        if o2 < 0 and -o2 < plus:
            out.append((1, 1))
        if o2 > 0 and o2 < minus:
            out.append((1, -1))
    return out


CHUNK, HOP, LEAD, STAGE, PART = 0.98, 1.7, 2.0, 2.2, 2.2


def schedule():
    links = [(axis, sign) for axis in (0, 1) for sign in (1, -1)]
    free = {link: 0.0 for link in links}
    queue = {link: [] for link in links}
    arrivals, ready, program = [], [(0.0, 0, "part")], []
    count, now = 0, 0.0

    def left(half, o1, o2, leg, sign):
        reach = FIRST[half] if leg == 0 else second(o1)
        gone = abs(o1) if leg == 0 else abs(o2)
        return reach[0 if sign > 0 else 1] - gone + (4 if leg == 0 else 0)

    def enqueue(half, o1, o2):
        nonlocal count
        for leg, sign in hops(half, o1, o2):
            count += 1
            item = (-left(half, o1, o2, leg, sign), count, half, o1, o2, leg, sign)
            heapq.heappush(queue[((half + leg) % 2, sign)], item)

    def burst(share, after):
        nonlocal count
        end = now
        for axis, sign in links:
            free[axis, sign] = max(now, free[axis, sign]) + 8 * share[axis] * CHUNK
            end = max(end, free[axis, sign])
        count += 1
        heapq.heappush(ready, (end + STAGE, count, after))

    def at(delay, *names):
        nonlocal count
        for name in names:
            count += 1
            heapq.heappush(ready, (now + delay, count, name))

    for half in (0, 1):
        enqueue(half, 0, 0)
    while True:
        if arrivals and arrivals[0][0] <= now:
            _, _, half, o1, o2 = heapq.heappop(arrivals)
            program.append(("wait", half, o1, o2))
            now += 0.04
            enqueue(half, o1, o2)
            continue
        open_links = [k for k in links if queue[k] and free[k] - now <= LEAD]
        if open_links:
            link = min(open_links, key=lambda k: free[k])
            _, _, half, o1, o2, leg, sign = heapq.heappop(queue[link])
            program.append(("send", half, o1, o2, leg, sign))
            free[link] = max(now, free[link]) + CHUNK
            seen = (o1 - sign, o2) if leg == 0 else (o1, o2 - sign)
            count += 1
            heapq.heappush(arrivals, (free[link] + HOP, count, half) + seen)
            now += 0.03
            continue
        if ready and ready[0][0] <= now:
            name = heapq.heappop(ready)[2]
            program.append((name,))
            if name == "part":
                now += PART
                burst((1 / 3, 1 / 3), "sum1")
                at(0.0, "targets")
            elif name == "targets":
                now += 0.6
                at(0.0, "self")
            elif name == "sum1":
                now += 0.3
                burst((1 / 24, 1 / 24), "sum2")
            elif name == "sum2":
                now += 0.2
                burst((1 / 24, 1 / 48), "sum3")
            elif name == "sum3":
                burst((1 / 6, 1 / 3), "own")
            elif name == "own":
                at(3.0, "far1")
                at(4.2, "relay1", "relay3")
                at(6.2, "rest1", "rest3")
                at(8.6, "last")
            elif name in ("rest1", "rest3"):
                at(0.2, "far" + {"rest1": "2", "rest3": "6"}[name])
                at(2.5, "far" + {"rest1": "3", "rest3": "7"}[name])
            elif name == "last":
                at(0.2, "far4")
                at(2.5, "far5")
            elif name in ("relay1", "relay3"):
                pass
            else:
                now += 0.36 if name == "self" else 0.72
            continue
        times = [free[k] - LEAD for k in links if queue[k]]
        times += [arrivals[0][0]] if arrivals else []
        times += [ready[0][0]] if ready else []
        if not times:
            return program, now
        now = max(now + 1e-3, min(times))


def slot_of(half, o1, o2):
    oz, oy = (o1, o2) if half == 0 else (o2, o1)
    return (oy % SIDE) * SIDE + oz % SIDE


def split3(v):
    hi = v.astype(BF).astype(F32)
    mid = (v - hi).astype(BF).astype(F32)
    return hi, mid, v - hi - mid


def aug_rows(v, first):
    hi, mid, lo = split3(v)
    row = lax.broadcasted_iota(jnp.int32, (16, v.shape[1]), 0)
    k = row - 3 * first
    terms = jnp.where(k == 0, hi, jnp.where(k == 1, mid, lo))
    mine = (k >= 0) & (k < 3)
    return jnp.where(mine, terms, jnp.where(row < 6, 1.0, 0.0)).astype(BF)


def half_norm(xt):
    xf = xt.astype(F32)
    return -0.5 * jnp.sum(xf * xf, axis=0, keepdims=True)


def kernel(
    near_hbm, count_hbm, index_hbm, pts_ref, wts_ref, interp_ref, out_ref,
    gat, interp_v, near_ref, count_ref, index_v, part, got1, mid_p, mid_w, got_p, got_w, skel, lhs, acc,
    loc, g_send, g_recv, s_send, s_recv, x_recv,
):
    grp, leaf = lax.axis_index("grp"), lax.axis_index("leaf")
    x, core = grp // 2, grp % 2
    y, z = leaf // SIDE, leaf % SIDE

    def at_leaf(oy, oz):
        return (grp, ((y + oy + SIDE) % SIDE) * SIDE + (z + oz + SIDE) % SIDE)

    def at_grp(ox, oc):
        return (((x + ox) % 4) * 2 + (core + oc) % 2, leaf)

    barrier = pltpu.get_barrier_semaphore()
    peers = [at_leaf(0, o) for o in range(1, SIDE)] + [at_leaf(o, 0) for o in range(1, SIDE)]
    peers += [at_grp(1, 0), at_grp(3, 0), at_grp(0, 1)]
    for peer in peers:
        pl.semaphore_signal(barrier, inc=1, device_id=peer, device_id_type=MESH)
    own = [
        pltpu.make_async_copy(pts_ref, gat.at[0, pl.ds(0, FEAT)], loc.at[0]),
        pltpu.make_async_copy(wts_ref, gat.at[0, pl.ds(FEAT, COLS)], loc.at[1]),
        pltpu.make_async_copy(interp_ref, interp_v, loc.at[2]),
        pltpu.make_async_copy(index_hbm, index_v, loc.at[3]),
        pltpu.make_async_copy(near_hbm, near_ref, loc.at[4]),
        pltpu.make_async_copy(count_hbm, count_ref, loc.at[5]),
    ]
    for c in own:
        c.start()
    pl.semaphore_wait(barrier, len(peers))

    def remote(src, dst, send, recv, peer):
        pltpu.make_async_remote_copy(
            src_ref=src, dst_ref=dst, send_sem=send, recv_sem=recv,
            device_id=peer, device_id_type=MESH,
        ).start()

    def whole(ref, sem):
        pltpu.make_async_copy(ref, ref, sem).wait()

    def do_send(half, o1, o2, leg, sign):
        here = slot_of(half, o1, o2)
        there = slot_of(half, *((o1 - sign, o2) if leg == 0 else (o1, o2 - sign)))
        rows = pl.ds(half * HALF, HALF)
        peer = at_leaf(0, sign) if (half + leg) % 2 == 0 else at_leaf(sign, 0)
        parts = [(gat.at[here, rows], rows)]
        if here == 0 and half == 0:
            parts = [(pts_ref.at[rows], rows)]
        elif here == 0:
            last, below = pl.ds(HALF, FEAT - HALF), pl.ds(FEAT, COLS)
            parts = [(pts_ref.at[last], last), (wts_ref, below)]
        for src, place in parts:
            remote(src, gat.at[there, place], g_send, g_recv.at[half, there], peer)

    def do_wait(half, o1, o2):
        here = slot_of(half, o1, o2)
        whole(gat.at[here, pl.ds(half * HALF, HALF)], g_recv.at[half, here])

    def scatter(kind, place):
        for o in FARTHEST:
            remote(part.at[kind, (place + o) % SIDE], got1.at[kind, 7 - o], s_send.at[0, kind],
                   s_recv.at[0, kind], peer_on(1 - kind, o))

    def do_part():
        for c in own[:4]:
            c.wait()
        index = index_v[...] - leaf * PTS
        pick = lax.broadcasted_iota(jnp.int32, (PTS, SKEL), 0) == index
        pts = jnp.dot(gat[0, :FEAT], pick.astype(BF), preferred_element_type=F32).astype(BF)
        for k in range(SIDE):
            part[0, k] = pts[:, k * PIECE:(k + 1) * PIECE]
        scatter(0, y)
        wts = jnp.dot(gat[0, FEAT:], interp_v[...], preferred_element_type=F32)
        hi = wts.astype(BF)
        lo = (wts - hi.astype(F32)).astype(BF)
        for k in range(SIDE):
            cols = slice(k * PIECE, (k + 1) * PIECE)
            part[1, k, :COLS] = hi[:, cols]
            part[1, k, COLS:] = lo[:, cols]
        scatter(1, z)

    takes = ((z, 2, y, FEAT // 16), (y, 4, z, COLS // 16))

    def peer_on(kind, o):
        return at_leaf(0, o) if kind == 0 else at_leaf(o, 0)

    def total(kind, first, got):
        v = first.astype(F32)
        for k in range(SIDE - 1):
            v = v + got[kind, k].astype(F32)
        return v if kind == 0 else v[:COLS] + v[COLS:]

    def do_sum1():
        for kind in (0, 1):
            whole(got1.at[kind], s_recv.at[0, kind])
        mid_p[...] = total(0, part[0, y], got1).astype(BF)
        mid_w[...] = total(1, part[1, z], got1)
        for kind, (mid, got) in enumerate(((mid_p, got_p), (mid_w, got_w))):
            place, every, _, chunks = takes[kind]
            for c in range(chunks):
                off = (every * c - place + SIDE) % SIDE

                @pl.when(off != 0)
                def _():
                    remote(mid.at[pl.ds(16 * c, 16)], got.at[SIDE - 1 - off], s_send.at[1, kind],
                           s_recv.at[1, kind], peer_on(kind, off))

    def do_sum2():
        for kind, (mid, got) in enumerate(((mid_p, got_p), (mid_w, got_w))):
            place, every, piece, _ = takes[kind]

            @pl.when(place % every == 0)
            def _():
                whole(got, s_recv.at[1, kind])
                row = pl.multiple_of(place // every * 16, 16)
                v = mid[pl.ds(row, 16)].astype(F32)
                for k in range(SIDE - 1):
                    v = v + got[k].astype(F32)
                mine = pl.ds(pl.multiple_of(kind * FEAT + row, 16), 16)
                skel[0, piece, mine] = v.astype(BF)
                for o in FARTHEST:
                    ref = skel.at[0, piece, mine]
                    remote(ref, ref, s_send.at[2, kind], s_recv.at[2, kind], peer_on(kind, o))

    def by_count(kind, one, sem):
        place, every, _, chunks = takes[kind]
        for here in (0, 1):
            @pl.when((place % every == 0) if here else (place % every != 0))
            def _():
                whole(one(chunks - here), sem)

    def do_sum3():
        for kind in (0, 1):
            by_count(kind, lambda n: skel.at[0, 0, pl.ds(0, 16 * n)], s_recv.at[2, kind])
        p, w = skel.at[0, y, pl.ds(0, FEAT)], skel.at[0, z, pl.ds(FEAT, COLS)]
        for o in FARTHEST:
            remote(p, p, s_send.at[4, 0], s_recv.at[3, 0], at_leaf(o, 0))
            remote(w, w, s_send.at[4, 1], s_recv.at[3, 1], at_leaf(0, o))

    others = (skel.at[0, pl.ds(0, 7), pl.ds(0, FEAT)], skel.at[0, pl.ds(0, 7), pl.ds(FEAT, COLS)])

    def hand_on(slot, part_of, k):
        remote(skel.at[slot, part_of], skel.at[slot + 1, part_of], s_send.at[3, 0],
               x_recv.at[slot + 1, k], at_grp(0, 1))

    halves = (pl.ds(0, 4), pl.ds(4, 4))

    def do_own():
        for kind in (0, 1):
            whole(others[kind], s_recv.at[3, kind])
        for first in (0, 1):
            for dx in (1, 3):
                there, k = 2 * (4 - dx), first if dx == 3 else 1 - first
                remote(skel.at[0, halves[k]], skel.at[there, halves[k]], s_send.at[3, 0],
                       x_recv.at[there, k], at_grp(dx, 0))
        for k in (0, 1):
            hand_on(0, halves[k], k)

    def do_relay(dx):
        k = 0 if dx == 1 else 1
        whole(skel.at[2 * dx, halves[k]], x_recv.at[2 * dx, k])
        remote(skel.at[2 * dx, halves[k]], skel.at[4, halves[k]], s_send.at[3, 1],
               x_recv.at[4, k], at_grp(4 - dx, 0))
        hand_on(2 * dx, halves[k], k)

    def do_rest(dx):
        k = 1 if dx == 1 else 0
        whole(skel.at[2 * dx, halves[k]], x_recv.at[2 * dx, k])
        hand_on(2 * dx, halves[k], k)

    def do_last():
        for k in (0, 1):
            whole(skel.at[4, halves[k]], x_recv.at[4, k])
            hand_on(4, halves[k], k)

    def block(xs, ws):
        rhs = jnp.concatenate([xs, aug_rows(half_norm(xs), 0)], axis=0)
        arg = jnp.dot(lhs[...], rhs, preferred_element_type=F32)
        kern = jnp.exp(arg).astype(BF)
        return lax.dot_general(kern, ws, (((1,), (1,)), ((), ())), preferred_element_type=F32)

    def do_targets():
        xt = gat[0, :FEAT]
        rows = jnp.concatenate([xt, aug_rows(half_norm(xt), 1)], axis=0)
        pad = jnp.zeros((128 - rows.shape[0], PTS), F32)
        turned = jnp.concatenate([rows.astype(F32), pad], axis=0).T
        lhs[...] = turned[:, :FEAT + 16].astype(BF)

    def do_self():
        acc[...] = block(gat[0, :FEAT], gat[0, FEAT:])

    def do_far(rel):
        if rel % 2 == 1:
            for k in (0, 1):
                whole(skel.at[rel, halves[k]], x_recv.at[rel, k])
        both = jnp.concatenate([skel[rel, i] for i in range(SIDE)], axis=1)
        acc[...] += (block(both[:FEAT, :PTS], both[FEAT:, :PTS])
                     + block(both[:FEAT, PTS:], both[FEAT:, PTS:]))

    work = {"wait": do_wait, "send": do_send, "part": do_part, "sum1": do_sum1,
            "sum2": do_sum2, "sum3": do_sum3, "own": do_own, "targets": do_targets, "self": do_self}
    for dx in (1, 3):
        work["relay%d" % dx] = functools.partial(do_relay, dx)
        work["rest%d" % dx] = functools.partial(do_rest, dx)
    work["last"] = do_last
    for rel in range(1, 8):
        work["far%d" % rel] = functools.partial(do_far, rel)
    for name, *args in schedule()[0]:
        work[name](*args)

    own[4].wait()
    own[5].wait()
    mine = count_ref[leaf]

    add = jnp.zeros((PTS, COLS), F32)
    for k in range(1, SLOTS):
        source = near_ref[k, leaf]
        sy = (source // SIDE + SIDE - y) % SIDE
        sz = (source % SIDE + SIDE - z) % SIDE
        got = gat[sy * SIDE + sz]
        used = jnp.where(k < mine, 1.0, 0.0).astype(F32)
        add = add + block(got[:FEAT], (got[FEAT:].astype(F32) * used).astype(BF))
    acc[...] += add

    pad = jnp.zeros((PTS, 128 - COLS), F32)
    out_ref[...] = jnp.concatenate([acc[...], pad], axis=1).T[:COLS]

    whole(gat.at[pl.ds(0, 63)], g_send)
    for kind in (0, 1):
        whole(got1.at[kind], s_send.at[0, kind])
        by_count(kind, lambda n: (mid_p, mid_w)[kind].at[pl.ds(0, 16 * n)], s_send.at[1, kind])
        place, every, _, _ = takes[kind]

        @pl.when(place % every == 0)
        def _():
            whole(skel.at[0, 0:7, pl.ds(0, 16)], s_send.at[2, kind])

        whole(others[kind], s_send.at[4, kind])
    whole(skel.at[pl.ds(0, 6)], s_send.at[3, 0])
    whole(skel.at[0], s_send.at[3, 1])


def per_device(points, weights, interp, near_leaf, near_count, skel_index):
    flops = 2 * 30 * PTS * PTS * (FEAT + 16 + COLS) + 2 * PTS * SKEL * ROWS
    given = (near_leaf.T, near_count, skel_index, points.T, weights.T, interp)
    out = pl.pallas_call(
        kernel,
        out_shape=jax.ShapeDtypeStruct((COLS, PTS), F32),
        in_specs=[pl.BlockSpec(memory_space=pltpu.HBM)] * 6,
        out_specs=pl.BlockSpec(memory_space=pltpu.VMEM),
        scratch_shapes=[
            pltpu.VMEM((64, ROWS, PTS), BF),
            pltpu.VMEM((PTS, SKEL), BF),
            pltpu.SMEM((SLOTS, 64), jnp.int32),
            pltpu.SMEM((64,), jnp.int32),
            pltpu.VMEM((1, SKEL), jnp.int32),
            pltpu.VMEM((2, SIDE, FEAT, PIECE), BF),
            pltpu.VMEM((2, SIDE - 1, FEAT, PIECE), BF),
            pltpu.VMEM((FEAT, PIECE), BF),
            pltpu.VMEM((COLS, PIECE), F32),
            pltpu.VMEM((SIDE - 1, 16, PIECE), BF),
            pltpu.VMEM((SIDE - 1, 16, PIECE), F32),
            pltpu.VMEM((8, SIDE, ROWS, PIECE), BF),
            pltpu.VMEM((PTS, FEAT + 16), BF),
            pltpu.VMEM((PTS, COLS), F32),
            pltpu.SemaphoreType.DMA((6,)),
            pltpu.SemaphoreType.DMA,
            pltpu.SemaphoreType.DMA((2, 64)),
            pltpu.SemaphoreType.DMA((5, 2)),
            pltpu.SemaphoreType.DMA((4, 2)),
            pltpu.SemaphoreType.DMA((8, 2)),
        ],
        cost_estimate=pl.CostEstimate(
            flops=flops, bytes_accessed=2 * PTS * SKEL, transcendentals=30 * PTS * PTS
        ),
        compiler_params=pltpu.CompilerParams(
            collective_id=0, has_side_effects=True, vmem_limit_bytes=40 * 1024 * 1024
        ),
    )(*[pltpu.with_memory_space_constraint(a, pltpu.HBM) for a in given])
    return out.T


def solution(mesh):
    placed = (
        P(("grp", "leaf"), None),
        P(("grp", "leaf"), None),
        P(("grp", "leaf"), None),
        P("grp", None),
        P("grp"),
        P("grp", None),
    )
    return jax.shard_map(
        per_device, mesh=mesh, in_specs=placed, out_specs=P(("grp", "leaf"), None), check_vma=False
    )
```
